256 devices in a mesh: rep: 16 (over x_lo, z), row: 8 (over y, core), col: 2 (over x_hi).
Axes of the slice: x: 4 (x_hi: 2, x_lo: 2; x = x_hi * 2 + x_lo), y: 4, z: 8, core: 2. Of those that a mesh axis runs over, the one named last changes fastest.
Arguments:
- design_rows: bfloat16 [16384, 49152], P('rep', ('row', 'col')), may hold values from -0.046875 to 0.046875
- design_panel: bfloat16 [16384, 2, 512], P('rep', 'col', 'row'), may hold values from -6 to 6
- observations: float32 [16384], P('rep'), may hold values from -6 to 6
- group_ids: int32 [16384], P('rep'), may hold values from 0 to 7
- group_sigma: float32 [8], replicated, may hold values from 0.5 to 2
Outputs:
- normal_panel: float32 [8, 2, 3072, 1024], P('row', None, 'rep', 'col')
- normal_rhs: float32 [8, 2, 3072], P('row', None, 'rep')
The draws below stay inside these ranges and needn't reach their ends.
All inputs are finite; a program needn't handle non-finite values.
Results may differ from the reference program's by a relative error of at most 0.0029.
Values may be sent and summed in bfloat16 or wider, within the bound.
No kernel may reach another device: no remote copies, remote signals or barrier semaphores. Data moves between devices by JAX's collectives and lax.ppermute only.
A program may use at most 128 MiB of HBM per device.

```python
import math
import jax
import jax.numpy as jnp
from jax import lax

COEFS = 49152
PANEL = 1024
GROUPS = 8
POINTS = 16384
SHARD_ROWS = 3072
N_ROW = 8
N_COL = 2


def touch_ends(array, stream_key, smallest, top_value):
    longest = array.shape.index(max(array.shape))
    spots = []
    for shift in (0, 1):
        where = [jax.random.randint(jax.random.fold_in(stream_key, axis), (), 0, length) for axis, length in enumerate(array.shape)]
        where[longest] = (where[longest] + shift) % array.shape[longest]
        spots.append(tuple(where))
    return array.at[spots[0]].set(smallest).at[spots[1]].set(top_value)


def block_scale(own_key, dims, pieces, smallest, high):
    level = 1.0
    for dim, shards_of in pieces:
        heights = jax.random.uniform(jax.random.fold_in(jax.random.fold_in(own_key, 6), dim), (shards_of,), jnp.float32, smallest / len(pieces), high / len(pieces))
        level = level * jnp.repeat(jnp.exp(heights), dims[dim] // shards_of).reshape((-1,) + (1,) * (len(dims) - 1 - dim))
    return level


def centred(own_key, extent, deviation, most, pieces=(), kind=jnp.bfloat16):
    level = block_scale(own_key, extent, pieces, -0.22, 0.18) if pieces else 1.0
    result = jax.random.normal(own_key, extent, jnp.float32) * deviation * level
    return jnp.minimum(jnp.maximum(result, -most), most).astype(kind)


def setup_inputs(seed: int = 0) -> dict:
    key_list = jax.random.split(jax.random.key(seed), 6)
    design_rows = centred(key_list[0], (POINTS, COEFS), POINTS ** -0.5, 0.046875, ((0, 16), (1, 16)))
    design_panel = centred(key_list[1], (POINTS, N_COL, PANEL // N_COL), 1.0, 6.0, ((0, 16), (1, 2), (2, 8)))
    observations = centred(key_list[2], (POINTS,), 1.0, 6.0, ((0, 16),), jnp.float32)
    group_ids = touch_ends(jax.random.randint(key_list[3], (POINTS,), 0, GROUPS), jax.random.fold_in(key_list[3], 1), 0, GROUPS - 1).astype(jnp.int32)
    group_sigma = jnp.clip(jnp.exp(jax.random.uniform(key_list[4], (GROUPS,), jnp.float32, math.log(0.5), math.log(2.0))), 0.5, 2.0)
    return dict(design_rows=design_rows, design_panel=design_panel, observations=observations, group_ids=group_ids, group_sigma=group_sigma)


def reference(design_rows, design_panel, observations, group_ids, group_sigma):
    sigma = group_sigma[group_ids]
    weights = 1.0 / (sigma * sigma)
    weighted_panel = (weights[:, None] * design_panel.reshape(POINTS, PANEL).astype(jnp.float32)).astype(jnp.bfloat16)
    weighted_obs = (weights * observations).astype(jnp.bfloat16)
    panel_f = weighted_panel.astype(jnp.float32)
    obs_f = weighted_obs.astype(jnp.float32)
    tiles = design_rows.reshape(POINTS, N_ROW, COEFS // N_ROW)

    def one_tile(index):
        tile_rows = lax.dynamic_index_in_dim(tiles, index, 1, keepdims=False).astype(jnp.float32)
        normal = jnp.dot(tile_rows.T, panel_f, precision=lax.Precision.HIGHEST)
        rhs_part = jnp.dot(tile_rows.T, obs_f, precision=lax.Precision.HIGHEST)
        return normal, rhs_part

    normal_all, rhs_all = lax.map(one_tile, jnp.arange(N_ROW, dtype=jnp.int32))
    normal_panel = normal_all.reshape(N_ROW, N_COL, SHARD_ROWS, PANEL)
    normal_rhs = rhs_all.reshape(N_ROW, N_COL, SHARD_ROWS)
    return normal_panel, normal_rhs
```

```python
import functools

import jax
import jax.numpy as jnp
from jax import lax
from jax.experimental import pallas as pl
from jax.experimental.pallas import tpu as pltpu
from jax.sharding import PartitionSpec as P

NZ = 8
ROWS = 192
PAIR = 2 * ROWS
HALF = 512
PART = 256
TAIL = 16
BF16, F32 = jnp.bfloat16, jnp.float32
IN_VMEM = pl.BlockSpec(memory_space=pltpu.VMEM)
IN_SMEM = pl.BlockSpec(memory_space=pltpu.SMEM)


def call(kernel, out_shape, n_in, scratch=(), flops=0, moved=0, limit=16, first=IN_SMEM):
    several = isinstance(out_shape, (list, tuple))
    return pl.pallas_call(
        kernel,
        out_shape=out_shape,
        in_specs=[first] + [IN_VMEM] * (n_in - 1),
        out_specs=[IN_VMEM] * len(out_shape) if several else IN_VMEM,
        scratch_shapes=list(scratch),
        compiler_params=pltpu.CompilerParams(vmem_limit_bytes=limit * 2**20),
        cost_estimate=pl.CostEstimate(
            flops=flops, bytes_accessed=moved, transcendentals=0
        ),
    )


def weigh_kernel(sigma_ref, panel_ref, obs_ref, ids_ref, panel_out, obs_out):
    ids = ids_ref[...]
    sigma = jnp.full(ids.shape, sigma_ref[0], F32)
    for g in range(1, sigma_ref.shape[0]):
        sigma = jnp.where(ids == g, sigma_ref[g], sigma)
    weights = 1.0 / (sigma * sigma)
    panel_out[...] = (weights * panel_ref[...].astype(F32)).astype(BF16)
    weighted = (weights * obs_ref[...]).astype(BF16)
    obs_out[...] = jnp.broadcast_to(weighted, obs_out.shape)


def weigh(panel_t, observations, group_ids, group_sigma):
    cols, points = panel_t.shape
    flat = pl.BlockSpec((1, points), lambda i: (0, 0))
    return pl.pallas_call(
        weigh_kernel,
        grid=(1,),
        out_shape=(
            jax.ShapeDtypeStruct((cols, points), BF16),
            jax.ShapeDtypeStruct((TAIL, points), BF16),
        ),
        in_specs=[IN_SMEM, pl.BlockSpec((cols, points), lambda i: (0, 0)), flat, flat],
        out_specs=[
            pl.BlockSpec((cols, points), lambda i: (0, 0)),
            pl.BlockSpec((TAIL, points), lambda i: (0, 0)),
        ],
    )(group_sigma, panel_t, observations.reshape(1, -1), group_ids.reshape(1, -1))


def pair_kernel(rows_ref, out_ref, held, sems):
    copies = []
    for e in range(NZ // 2):
        for a in range(2):
            n = a * (NZ // 2) + e
            copies.append(
                pltpu.make_async_copy(
                    rows_ref.at[:, n * PAIR : (n + 1) * PAIR], held.at[n], sems.at[n]
                )
            )
            copies[-1].start()
    for e in range(NZ // 2):
        copies[2 * e].wait()
        copies[2 * e + 1].wait()
        for half in range(2):
            lanes = slice(half * ROWS, (half + 1) * ROWS)
            out_ref[2 * e + half] = jnp.concatenate(
                [held[e, :, lanes], held[NZ // 2 + e, :, lanes]], axis=1
            )


def pair_up(design_rows):
    points = design_rows.shape[0]
    return call(
        pair_kernel,
        jax.ShapeDtypeStruct((NZ, points, PAIR), BF16),
        1,
        scratch=[pltpu.VMEM((NZ, points, PAIR), BF16), pltpu.SemaphoreType.DMA((NZ,))],
        moved=4 * design_rows.size,
        limit=12,
        first=pl.BlockSpec(memory_space=pl.ANY),
    )(design_rows)


def product(left, right):
    return jnp.dot(left, right, preferred_element_type=F32)


def plus(total, received):
    main = total[:-TAIL] + received[:-TAIL, :].astype(F32)
    tail = received[-TAIL:, :].astype(F32)
    more = tail[: TAIL // 2] + tail[TAIL // 2 :]
    return jnp.concatenate([main, total[-TAIL:] + jnp.concatenate([more, more], axis=0)], axis=0)


def packed(total):
    high = total[-TAIL : -TAIL // 2].astype(BF16).astype(F32)
    low = total[-TAIL // 2 :] - high
    main = [total[:-TAIL]] if total.shape[0] > TAIL else []
    return jnp.concatenate(main + [high, low], axis=0).astype(BF16)


def place(meta_ref, dz):
    return (meta_ref[0] + dz) & (NZ - 1)


def x_rows(panel_ref, which):
    at = pl.multiple_of(which * PART, PART)
    return jnp.concatenate([panel_ref[pl.ds(at, PART), :], panel_ref[HALF:, :]], axis=0)


def z_kernel(steps, meta_ref, rows_ref, panel_ref, *refs):
    received, outs = refs[: -len(steps)], refs[-len(steps) :]
    left = panel_ref[...]
    for i, dz in enumerate(steps):
        total = product(left, rows_ref[place(meta_ref, dz)])
        if i < len(received):
            total = plus(total, received[i])
        outs[i][...] = packed(total)


def z_step(meta, rows, panel, steps, received):
    shape = (panel.shape[0], PAIR)
    n = len(steps)
    return call(
        functools.partial(z_kernel, steps),
        [jax.ShapeDtypeStruct(shape, BF16)] * n,
        3 + len(received),
        flops=2 * n * shape[0] * PAIR * rows.shape[1],
        moved=2 * n * (rows.shape[1] * PAIR + 2 * shape[0] * PAIR),
    )(meta, rows, panel, *received)


def over_kernel(steps, meta_ref, rows_ref, panel_ref, out_ref):
    left = x_rows(panel_ref, 1 - meta_ref[1])
    for i, dz in enumerate(steps):
        out_ref[i] = packed(product(left, rows_ref[place(meta_ref, dz)]))


def over_x(meta, rows, panel, steps):
    shape = (len(steps), PART + TAIL, PAIR)
    return call(
        functools.partial(over_kernel, steps),
        jax.ShapeDtypeStruct(shape, BF16),
        3,
        flops=2 * len(steps) * shape[1] * PAIR * rows.shape[1],
        moved=2 * len(steps) * (rows.shape[1] * PAIR + shape[1] * PAIR),
    )(meta, rows, panel)


def x_kernel(steps, picks, n_over, meta_ref, rows_ref, panel_ref, *refs):
    over, refs = refs[:n_over], refs[n_over:]
    received, outs = refs[: -len(steps)], refs[-len(steps) :]
    left = x_rows(panel_ref, meta_ref[1])
    for i, dz in enumerate(steps):
        total = product(left, rows_ref[place(meta_ref, dz)])
        which, at = picks[i]
        total = plus(total, over[which].at[at])
        if i < len(received):
            total = plus(total, received[i])
        outs[i][...] = packed(total)


def x_step(meta, rows, panel, steps, over, received):
    arrays, picks = [], []
    for dz in steps:
        array, at = over[dz]
        known = [a is array for a in arrays]
        if not any(known):
            known.append(True)
            arrays.append(array)
        picks.append((known.index(True), at))
    shape = (PART + TAIL, PAIR)
    n = len(steps)
    return call(
        functools.partial(x_kernel, steps, tuple(picks), len(arrays)),
        [jax.ShapeDtypeStruct(shape, BF16)] * n,
        3 + len(arrays) + len(received),
        flops=2 * n * shape[0] * PAIR * rows.shape[1],
        moved=2 * n * (rows.shape[1] * PAIR + 3 * shape[0] * PAIR),
    )(meta, rows, panel, *arrays, *received)


def widened(tail, width):
    zeros = jnp.zeros((tail.shape[0], width - tail.shape[1]), tail.dtype)
    return jnp.concatenate([tail, zeros], axis=1)


def z_last_kernel(meta_ref, rows_ref, panel_ref, down, up, own_ref, rhs_ref, sent_ref, turned):
    side = meta_ref[1]
    total = product(panel_ref[...], rows_ref[meta_ref[0]])
    total = plus(plus(total, down), up)
    turned[...] = total[:HALF].T
    own_ref[...] = turned[pl.ds(pl.multiple_of(side * ROWS, ROWS), ROWS), :]
    sent_ref[:ROWS, :] = turned[
        pl.ds(pl.multiple_of((1 - side) * ROWS, ROWS), ROWS), :
    ].astype(BF16)
    tail = total[HALF:]
    lower, upper = tail[:, :ROWS], tail[:, ROWS:]
    rhs_ref[...] = jnp.where(side == 0, lower, upper)[: TAIL // 2]
    other = packed(jnp.where(side == 0, upper, lower))
    sent_ref[ROWS:, :] = widened(other.astype(F32), HALF).astype(BF16)


def z_last(meta, rows, panel, down, up):
    return call(
        z_last_kernel,
        [
            jax.ShapeDtypeStruct((ROWS, HALF), F32),
            jax.ShapeDtypeStruct((TAIL // 2, ROWS), F32),
            jax.ShapeDtypeStruct((ROWS + TAIL, HALF), BF16),
        ],
        5,
        scratch=[pltpu.VMEM((PAIR, HALF), F32)],
        flops=2 * panel.shape[0] * PAIR * rows.shape[1],
        moved=4 * rows.shape[1] * PAIR,
    )(meta, rows, panel, down, up)


def x_last_kernel(at, meta_ref, rows_ref, panel_ref, over, up, down, near_ref, cross_ref, turned):
    side = meta_ref[1]
    total = product(x_rows(panel_ref, side), rows_ref[meta_ref[0]])
    total = plus(plus(plus(total, over.at[at]), up), down)
    turned[...] = total[:PART].T
    near_ref[...] = turned[pl.ds(pl.multiple_of(side * ROWS, ROWS), ROWS), :]
    cross_ref[:ROWS, :] = turned[pl.ds(pl.multiple_of((1 - side) * ROWS, ROWS), ROWS), :]
    tail = total[PART:]
    other = jnp.where(side == 0, tail[:, ROWS:], tail[:, :ROWS])[: TAIL // 2]
    cross_ref[ROWS:, :] = widened(other, PART)


def x_last(meta, rows, panel, over, up, down):
    array, at = over
    return call(
        functools.partial(x_last_kernel, at),
        [
            jax.ShapeDtypeStruct((ROWS, PART), F32),
            jax.ShapeDtypeStruct((ROWS + TAIL // 2, PART), F32),
        ],
        6,
        scratch=[pltpu.VMEM((PAIR, PART), F32)],
        flops=2 * (PART + TAIL) * PAIR * rows.shape[1],
        moved=4 * rows.shape[1] * PAIR,
    )(meta, rows, panel, array, up, down)


def finish_kernel(meta_ref, own_ref, rhs_ref, part_ref, near_ref, cross_ref, out_ref, rhs_out):
    side, y, core, half = meta_ref[1], meta_ref[2], meta_ref[3], meta_ref[4]
    own = own_ref[...] + part_ref[:ROWS, :].astype(F32)
    near, cross = near_ref[...], cross_ref[:ROWS, :]
    first = jnp.where(side == 0, near, cross)
    second = jnp.where(side == 0, cross, near)
    for where_to, left, right in (
        (half, own[:, :PART], own[:, PART:]),
        (1 - half, first, second),
    ):
        mine = jnp.where(core == 0, left, right)
        other = jnp.where(core == 0, right, left)
        for dy in range(4):
            lanes = slice(dy * 64, dy * 64 + 64)
            at = pl.multiple_of(((y + dy) & 3) * 128, 128)
            out_ref[0, where_to, :, pl.ds(at, 128)] = jnp.concatenate(
                [mine[:, lanes], other[:, lanes]], axis=1
            )
    tail = part_ref[ROWS:, :].astype(F32)[:, :ROWS]
    mine = (rhs_ref[...] + (tail[: TAIL // 2] + tail[TAIL // 2 :]))[:1]
    other = cross_ref[ROWS:, :][:1, :ROWS]
    rhs_out[0] = jnp.concatenate(
        [jnp.where(half == 0, mine, other), jnp.where(half == 0, other, mine)], axis=0
    )


def finish(meta, own, rhs, part, near, cross):
    return call(
        finish_kernel,
        [
            jax.ShapeDtypeStruct((1, 2, ROWS, HALF), F32),
            jax.ShapeDtypeStruct((1, 2, ROWS), F32),
        ],
        6,
        moved=6 * 2**20,
    )(meta, own, rhs, part, near, cross)


def z_shift(x, d):
    return lax.ppermute(
        x, "rep", [(a * NZ + z, a * NZ + (z + d) % NZ) for a in range(2) for z in range(NZ)]
    )


def x_swap(x):
    return lax.ppermute(
        x, "rep", [(a * NZ + z, (1 - a) * NZ + z) for a in range(2) for z in range(NZ)]
    )


def y_shift(x, d):
    return lax.ppermute(
        x, "row", [(y * 2 + c, (y + d) % 4 * 2 + c) for y in range(4) for c in range(2)]
    )


def core_swap(x):
    return lax.ppermute(x, "row", [(i, i ^ 1) for i in range(8)])


def half_swap(x):
    return lax.ppermute(x, "col", [(0, 1), (1, 0)])


def cross_swap(x):
    pairs = []
    for a in range(2):
        for z in range(NZ):
            for h in range(2):
                pairs.append(((a * NZ + z) * 2 + h, ((1 - a) * NZ + z) * 2 + 1 - h))
    return lax.ppermute(x, ("rep", "col"), pairs)


def per_device(design_rows, design_panel, observations, group_ids, group_sigma):
    rep, row, half = (lax.axis_index(n) for n in ("rep", "row", "col"))
    meta = jnp.stack([rep & (NZ - 1), rep >> 3, row >> 1, row & 1, half]).astype(jnp.int32)
    points = design_rows.shape[0]
    panel_t = jnp.transpose(design_panel.reshape(points, -1))
    mine, weighted_obs = weigh(panel_t, observations, group_ids, group_sigma)
    rows = pair_up(design_rows)

    def along_y(block):
        near = jnp.concatenate([block] + [y_shift(block, -d) for d in (1, 2, 3)], axis=0)
        return jnp.concatenate([near, core_swap(near), weighted_obs], axis=0)

    foreign = half_swap(mine)
    panel_z = along_y(mine)
    panel_x = along_y(foreign)

    over = {}
    for piece in ((4,), (3, -3), (2, -2), (1, -1, 0)):
        got = x_swap(over_x(meta, rows, panel_x, piece))
        for i, dz in enumerate(piece):
            over[dz] = (got, i)

    z_got, x_got = (), ()
    for s in (4, 3, 2, 1):
        steps = (-s,) if s == 4 else (-s, s)
        sent = z_step(meta, rows, panel_z, steps, z_got)
        z_got = (z_shift(sent[0], -1),) + tuple(z_shift(v, 1) for v in sent[1:])
        steps = (s,) if s == 4 else (s, -s)
        sent = x_step(meta, rows, panel_x, steps, over, x_got)
        x_got = (z_shift(sent[0], 1),) + tuple(z_shift(v, -1) for v in sent[1:])

    own, rhs, sent = z_last(meta, rows, panel_z, *z_got)
    part = x_swap(sent)
    near, cross = x_last(meta, rows, panel_x, over[0], *x_got)
    near, cross = half_swap(near), cross_swap(cross)
    return finish(meta, own, rhs, part, near, cross)


def solution(mesh):
    in_specs = (P("rep", ("row", "col")), P("rep", "col", "row"), P("rep"), P("rep"), P())
    out_specs = (P("row", None, "rep", "col"), P("row", None, "rep"))
    return jax.shard_map(
        per_device, mesh=mesh, in_specs=in_specs, out_specs=out_specs, check_vma=False
    )
```

```python
import functools

import jax
import jax.numpy as jnp
from jax import lax
from jax.experimental import pallas as pl
from jax.experimental.pallas import tpu as pltpu
from jax.sharding import PartitionSpec as P

NZ = 8
ROWS = 192
PAIR = 2 * ROWS
HALF = 512
PART = 256
TAIL = 16
BF16, F32 = jnp.bfloat16, jnp.float32
IN_VMEM = pl.BlockSpec(memory_space=pltpu.VMEM)
IN_SMEM = pl.BlockSpec(memory_space=pltpu.SMEM)


def call(kernel, out_shape, args, after=(), scratch=(), cost=4e9):
    n, extra = len(args), len(after)

    def body(*refs):
        kernel(*refs[:n], *refs[n + extra :])

    return pl.pallas_call(
        body,
        out_shape=out_shape,
        in_specs=[IN_SMEM] + [IN_VMEM] * (n - 1 + extra),
        out_specs=[IN_VMEM] * len(out_shape),
        scratch_shapes=list(scratch),
        compiler_params=pltpu.CompilerParams(vmem_limit_bytes=16 * 2**20),
        cost_estimate=pl.CostEstimate(flops=int(cost), bytes_accessed=1, transcendentals=0),
    )(*args, *after)


def weigh_kernel(sigma_ref, panel_ref, obs_ref, ids_ref, panel_out, obs_out):
    ids = ids_ref[...]
    sigma = jnp.full(ids.shape, sigma_ref[0], F32)
    for g in range(1, sigma_ref.shape[0]):
        sigma = jnp.where(ids == g, sigma_ref[g], sigma)
    weights = 1.0 / (sigma * sigma)
    panel_out[...] = (weights * panel_ref[...].astype(F32)).astype(BF16)
    weighted = (weights * obs_ref[...]).astype(BF16)
    obs_out[...] = jnp.broadcast_to(weighted, obs_out.shape)


def weigh(panel_t, observations, group_ids, group_sigma):
    cols, points = panel_t.shape
    flat = pl.BlockSpec((1, points), lambda i: (0, 0))
    return pl.pallas_call(
        weigh_kernel,
        grid=(1,),
        out_shape=(
            jax.ShapeDtypeStruct((cols, points), BF16),
            jax.ShapeDtypeStruct((TAIL, points), BF16),
        ),
        in_specs=[IN_SMEM, pl.BlockSpec((cols, points), lambda i: (0, 0)), flat, flat],
        out_specs=[IN_VMEM, IN_VMEM],
    )(group_sigma, panel_t, observations.reshape(1, -1), group_ids.reshape(1, -1))


def pair_kernel(meta_ref, first_ref, second_ref, out_ref):
    e = pl.program_id(0)
    for half in range(2):
        lanes = slice(half * ROWS, (half + 1) * ROWS)
        out_ref[2 * e + half] = jnp.concatenate(
            [first_ref[:, lanes], second_ref[:, lanes]], axis=1
        )


def pair_up(meta, design_rows):
    points = design_rows.shape[0]
    return pl.pallas_call(
        pair_kernel,
        grid=(NZ // 2,),
        out_shape=jax.ShapeDtypeStruct((NZ, points, PAIR), BF16),
        in_specs=[
            IN_SMEM,
            pl.BlockSpec((points, PAIR), lambda e: (0, e)),
            pl.BlockSpec((points, PAIR), lambda e: (0, e + NZ // 2)),
        ],
        out_specs=IN_VMEM,
        compiler_params=pltpu.CompilerParams(vmem_limit_bytes=12 * 2**20),
        cost_estimate=pl.CostEstimate(
            flops=0, bytes_accessed=4 * design_rows.size, transcendentals=0
        ),
    )(meta, design_rows, design_rows)


def collect_kernel(meta_ref, *refs):
    at = 0
    for ref in refs[:-1]:
        refs[-1][at : at + ref.shape[0], :] = ref[...]
        at += ref.shape[0]


def collect(meta, blocks, after):
    rows = sum(b.shape[0] for b in blocks)
    return call(
        collect_kernel,
        [jax.ShapeDtypeStruct((rows, blocks[0].shape[1]), BF16)],
        (meta, *blocks),
        after,
        cost=1e9,
    )[0]


def product(left, right):
    return jnp.dot(left, right, preferred_element_type=F32)


def plus(total, received):
    return total + received[...].astype(F32)


def plus_tailed(total, received):
    main = total[:-TAIL] + received[:-TAIL, :].astype(F32)
    tail = received[-TAIL:, :].astype(F32)
    more = tail[: TAIL // 2] + tail[TAIL // 2 :]
    return jnp.concatenate([main, total[-TAIL:] + jnp.concatenate([more, more], axis=0)], axis=0)


def split(value):
    high = value.astype(BF16).astype(F32)
    return high, value - high


def packed(total):
    high, low = split(total[-TAIL // 2 :])
    return jnp.concatenate([total[:-TAIL], high, low], axis=0).astype(BF16)


def place(meta_ref, dz):
    return (meta_ref[0] + dz) & (NZ - 1)


def x_rows(panel_ref, which):
    at = pl.multiple_of(which * PART, PART)
    return jnp.concatenate([panel_ref[pl.ds(at, PART), :], panel_ref[HALF:, :]], axis=0)


def z_kernel(steps, meta_ref, rows_ref, panel_ref, *refs):
    received, outs = refs[: -len(steps)], refs[-len(steps) :]
    left = panel_ref[:HALF, :]
    for i, dz in enumerate(steps):
        total = product(left, rows_ref[place(meta_ref, dz)])
        if i < len(received):
            total = plus(total, received[i])
        outs[i][...] = total.astype(BF16)


def z_step(meta, rows, panel, steps, received, after):
    return call(
        functools.partial(z_kernel, steps),
        [jax.ShapeDtypeStruct((HALF, PAIR), BF16)] * len(steps),
        (meta, rows, panel, *received),
        after,
    )


def over_kernel(steps, meta_ref, rows_ref, panel_ref, out_ref):
    left = x_rows(panel_ref, 1 - meta_ref[1])
    for i, dz in enumerate(steps):
        out_ref[i] = packed(product(left, rows_ref[place(meta_ref, dz)]))


def over_x(meta, rows, panel, steps, after):
    return call(
        functools.partial(over_kernel, steps),
        [jax.ShapeDtypeStruct((len(steps), PART + TAIL, PAIR), BF16)],
        (meta, rows, panel),
        after,
    )


def x_kernel(steps, picks, n_over, meta_ref, rows_ref, panel_ref, *refs):
    over, refs = refs[:n_over], refs[n_over:]
    received, outs = refs[: -len(steps)], refs[-len(steps) :]
    left = x_rows(panel_ref, meta_ref[1])
    for i, dz in enumerate(steps):
        total = product(left, rows_ref[place(meta_ref, dz)])
        which, at = picks[i]
        total = plus_tailed(total, over[which].at[at])
        if i < len(received):
            total = plus_tailed(total, received[i])
        outs[i][...] = packed(total)


def x_step(meta, rows, panel, steps, over, received, after):
    arrays, picks = [], []
    for dz in steps:
        array, at = over[dz]
        known = [a is array for a in arrays]
        if not any(known):
            known.append(True)
            arrays.append(array)
        picks.append((known.index(True), at))
    return call(
        functools.partial(x_kernel, steps, tuple(picks), len(arrays)),
        [jax.ShapeDtypeStruct((PART + TAIL, PAIR), BF16)] * len(steps),
        (meta, rows, panel, *arrays, *received),
        after,
    )


def halves(total):
    cols = total.shape[0]
    return [
        jnp.concatenate([total[c : c + 64] for c in range(first, cols, 128)], axis=0).T
        for first in (0, 64)
    ]


def last_kernel(
    at, meta_ref, rows_ref, near_ref, other_ref, over, x_up, x_down, z_down, z_up,
    own_x, own_z, rhs, beside, cross, across, x_this, x_that, z_this, z_that,
):
    side = meta_ref[1]
    right = rows_ref[meta_ref[0]]
    total = product(x_rows(near_ref, side), right)
    total = plus_tailed(plus_tailed(plus_tailed(total, over.at[at]), x_up), x_down)
    x_this[...], x_that[...] = halves(total[:PART])
    tail = total[PART:]
    total = plus(plus(product(other_ref[:HALF, :], right), z_down), z_up)
    z_this[...], z_that[...] = halves(total)
    mine = pl.ds(pl.multiple_of(side * ROWS, ROWS), ROWS)
    theirs = pl.ds(pl.multiple_of((1 - side) * ROWS, ROWS), ROWS)
    own_x[...] = x_this[mine, :]
    own_z[...] = z_this[mine, :]
    for out, x, z, where in (
        (beside, x_this, z_this, theirs),
        (cross, x_that, z_that, theirs),
        (across, x_that, z_that, mine),
    ):
        high, low = split(x[where, :])
        out[:ROWS, :] = jnp.concatenate([high, low, z[where, :]], axis=1).astype(BF16)
    lower, upper = tail[: TAIL // 2, :ROWS], tail[: TAIL // 2, ROWS:]
    rhs[...] = jnp.where(side == 0, lower, upper)
    high, low = split(jnp.where(side == 0, upper, lower))
    sent = jnp.concatenate([high, low], axis=0)
    zeros = jnp.zeros((TAIL, HALF - ROWS), F32)
    cross[ROWS:, :] = jnp.concatenate([sent, zeros], axis=1).astype(BF16)


def last(meta, rows, near, other, over, x_got, z_got, after):
    array, at = over
    message = jax.ShapeDtypeStruct((ROWS, HALF), BF16)
    return call(
        functools.partial(last_kernel, at),
        [
            jax.ShapeDtypeStruct((ROWS, PART // 2), F32),
            jax.ShapeDtypeStruct((ROWS, PART), F32),
            jax.ShapeDtypeStruct((TAIL // 2, ROWS), F32),
            message,
            jax.ShapeDtypeStruct((ROWS + TAIL, HALF), BF16),
            message,
        ],
        (meta, rows, near, other, array, *x_got, *z_got),
        after,
        scratch=[pltpu.VMEM((PAIR, n), F32) for n in (PART // 2, PART // 2, PART, PART)],
    )


def parts(message_ref):
    value = message_ref[:ROWS, :].astype(F32)
    quarter = HALF // 4
    return value[:, :quarter] + value[:, quarter : 2 * quarter], value[:, 2 * quarter :]


def finish_kernel(
    meta_ref, own_x, own_z, rhs_ref, beside_ref, cross_ref, across_ref, out_ref, rhs_out
):
    side, y, core, half = meta_ref[1], meta_ref[2], meta_ref[3], meta_ref[4]
    (beside_x, beside_z), (cross_x, cross_z), (across_x, across_z) = (
        parts(r) for r in (beside_ref, cross_ref, across_ref)
    )
    for where_to, here, there, other in (
        (half, own_x[...], beside_x, own_z[...] + beside_z),
        (1 - half, across_x, cross_x, cross_z + across_z),
    ):
        near = jnp.concatenate(
            [jnp.where(side == 0, here, there), jnp.where(side == 0, there, here)], axis=1
        )
        first = jnp.where(core == 0, near, other)
        second = jnp.where(core == 0, other, near)
        for dy in range(4):
            lanes = slice(dy * 64, dy * 64 + 64)
            at = pl.multiple_of(((y + dy) & 3) * 128, 128)
            out_ref[0, where_to, :, pl.ds(at, 128)] = jnp.concatenate(
                [first[:, lanes], second[:, lanes]], axis=1
            )
    tail = cross_ref[ROWS:, :].astype(F32)[:, :ROWS]
    mine = rhs_ref[...][:1]
    other = (tail[: TAIL // 2] + tail[TAIL // 2 :])[:1]
    rhs_out[0] = jnp.concatenate(
        [jnp.where(half == 0, mine, other), jnp.where(half == 0, other, mine)], axis=0
    )


def finish(meta, *args):
    return call(
        finish_kernel,
        [
            jax.ShapeDtypeStruct((1, 2, ROWS, HALF), F32),
            jax.ShapeDtypeStruct((1, 2, ROWS), F32),
        ],
        (meta, *args),
    )


def z_shift(x, d):
    return lax.ppermute(
        x, "rep", [(a * NZ + z, a * NZ + (z + d) % NZ) for a in range(2) for z in range(NZ)]
    )


def x_swap(x):
    return lax.ppermute(
        x, "rep", [(a * NZ + z, (1 - a) * NZ + z) for a in range(2) for z in range(NZ)]
    )


def y_shift(x, d):
    return lax.ppermute(
        x, "row", [(y * 2 + c, (y + d) % 4 * 2 + c) for y in range(4) for c in range(2)]
    )


def core_swap(x):
    return lax.ppermute(x, "row", [(i, i ^ 1) for i in range(8)])


def half_swap(x):
    return lax.ppermute(x, "col", [(0, 1), (1, 0)])


def cross_swap(x):
    pairs = []
    for a in range(2):
        for z in range(NZ):
            for h in range(2):
                pairs.append(((a * NZ + z) * 2 + h, ((1 - a) * NZ + z) * 2 + 1 - h))
    return lax.ppermute(x, ("rep", "col"), pairs)


def per_device(design_rows, design_panel, observations, group_ids, group_sigma):
    rep, row, half = (lax.axis_index(n) for n in ("rep", "row", "col"))
    meta = jnp.stack([rep & (NZ - 1), rep >> 3, row >> 1, row & 1, half]).astype(jnp.int32)
    points = design_rows.shape[0]
    panel_t = jnp.transpose(design_panel.reshape(points, -1))
    mine, weighted_obs = weigh(panel_t, observations, group_ids, group_sigma)
    rows = pair_up(meta, design_rows)

    foreign = half_swap(mine)
    blocks = [mine, foreign]
    for d in (1, 2, 3):
        blocks.append(y_shift(mine, -d))
    for d in (1, 2, 3):
        blocks.append(y_shift(foreign, -d))
    near = collect(meta, blocks[:2] + [blocks[i] for i in (2, 5, 3, 6, 4, 7)] + [weighted_obs], (rows,))
    other = core_swap(near)

    over, z_got, x_got, after = {}, (), (), ()

    def piece(*steps):
        nonlocal after
        (sent,) = over_x(meta, rows, near, steps, after)
        after = (sent,)
        got = x_swap(sent)
        for i, dz in enumerate(steps):
            over[dz] = (got, i)

    def z_next(s):
        nonlocal after, z_got
        steps = (-s,) if s == 4 else (-s, s)
        sent = z_step(meta, rows, other, steps, z_got, after)
        after = (sent[0],)
        z_got = (z_shift(sent[0], -1),) + tuple(z_shift(v, 1) for v in sent[1:])

    def x_next(s):
        nonlocal after, x_got
        steps = (s,) if s == 4 else (s, -s)
        sent = x_step(meta, rows, near, steps, over, x_got, after)
        after = (sent[0],)
        x_got = (z_shift(sent[0], 1),) + tuple(z_shift(v, -1) for v in sent[1:])

    piece(4)
    piece(3, -3)
    z_next(4)
    x_next(4)
    piece(2, -2)
    piece(1, -1, 0)
    z_next(3)
    x_next(3)
    z_next(2)
    x_next(2)
    z_next(1)
    x_next(1)
    own_x, own_z, rhs_own, beside, cross, across = last(
        meta, rows, near, other, over[0], x_got, z_got, after
    )
    return finish(
        meta, own_x, own_z, rhs_own, x_swap(beside), cross_swap(cross), half_swap(across)
    )


def solution(mesh):
    in_specs = (P("rep", ("row", "col")), P("rep", "col", "row"), P("rep"), P("rep"), P())
    out_specs = (P("row", None, "rep", "col"), P("row", None, "rep"))
    return jax.shard_map(
        per_device, mesh=mesh, in_specs=in_specs, out_specs=out_specs, check_vma=False
    )
```

```python
import functools

import jax
import jax.numpy as jnp
from jax import lax
from jax.experimental import pallas as pl
from jax.experimental.pallas import tpu as pltpu
from jax.sharding import PartitionSpec as P

NZ = 8
ROWS = 192
PAIR = 2 * ROWS
HALF = 512
PART = 256
TAIL = 16
BF16, F32 = jnp.bfloat16, jnp.float32
IN_VMEM = pl.BlockSpec(memory_space=pltpu.VMEM)
IN_SMEM = pl.BlockSpec(memory_space=pltpu.SMEM)


def call(kernel, out_shape, args, after=(), scratch=(), cost=4e9):
    n, extra = len(args), len(after)

    def body(*refs):
        kernel(*refs[:n], *refs[n + extra :])

    return pl.pallas_call(
        body,
        out_shape=out_shape,
        in_specs=[IN_VMEM] * (n + extra),
        out_specs=[IN_VMEM] * len(out_shape),
        scratch_shapes=list(scratch),
        compiler_params=pltpu.CompilerParams(vmem_limit_bytes=16 * 2**20),
        cost_estimate=pl.CostEstimate(flops=int(cost), bytes_accessed=1, transcendentals=0),
    )(*args, *after)


def weigh_kernel(sigma_ref, obs_ref, ids_ref, weights_out, obs_out):
    ids = ids_ref[...]
    sigma = jnp.full(ids.shape, sigma_ref[0], F32)
    for g in range(1, sigma_ref.shape[0]):
        sigma = jnp.where(ids == g, sigma_ref[g], sigma)
    weights = 1.0 / (sigma * sigma)
    weights_out[...] = jnp.broadcast_to(weights, weights_out.shape)
    weighted = (weights * obs_ref[...]).astype(BF16)
    obs_out[...] = jnp.broadcast_to(weighted, obs_out.shape)


def weigh(observations, group_ids, group_sigma):
    points = observations.shape[0]
    flat = pl.BlockSpec((1, points), lambda i: (0, 0))
    return pl.pallas_call(
        weigh_kernel,
        grid=(1,),
        out_shape=(
            jax.ShapeDtypeStruct((8, points), F32),
            jax.ShapeDtypeStruct((TAIL, points), BF16),
        ),
        in_specs=[IN_SMEM, flat, flat],
        out_specs=[IN_VMEM, IN_VMEM],
        compiler_params=pltpu.CompilerParams(vmem_limit_bytes=2 * 2**20),
    )(group_sigma, observations.reshape(1, -1), group_ids.reshape(1, -1))


def pair_kernel(first_ref, second_ref, out_ref):
    e = pl.program_id(0)
    for half in range(2):
        lanes = slice(half * ROWS, (half + 1) * ROWS)
        out_ref[2 * e + half] = jnp.concatenate(
            [first_ref[:, lanes], second_ref[:, lanes]], axis=1
        )


def pair_up(design_rows):
    points = design_rows.shape[0]
    return pl.pallas_call(
        pair_kernel,
        grid=(NZ // 2,),
        out_shape=jax.ShapeDtypeStruct((NZ, points, PAIR), BF16),
        in_specs=[
            pl.BlockSpec((points, PAIR), lambda e: (0, e)),
            pl.BlockSpec((points, PAIR), lambda e: (0, e + NZ // 2)),
        ],
        out_specs=IN_VMEM,
        compiler_params=pltpu.CompilerParams(vmem_limit_bytes=12 * 2**20),
        cost_estimate=pl.CostEstimate(
            flops=0, bytes_accessed=4 * design_rows.size, transcendentals=0
        ),
    )(design_rows, design_rows)


def collect_kernel(weights_ref, obs_ref, *refs):
    weights = weights_ref[:1, :]
    out, at = refs[-1], 0
    for ref in refs[:-1]:
        value = weights * ref[...].astype(F32)
        out[at : at + ref.shape[0], :] = value.astype(BF16)
        at += ref.shape[0]
    out[at:, :] = obs_ref[...]


def collect(weights, weighted_obs, blocks, after):
    rows = sum(b.shape[0] for b in blocks) + weighted_obs.shape[0]
    return call(
        collect_kernel,
        [jax.ShapeDtypeStruct((rows, weights.shape[1]), BF16)],
        (weights, weighted_obs, *blocks),
        after,
        cost=1e9,
    )[0]


def product(left, right):
    return jnp.dot(left, right, preferred_element_type=F32)


def plus(total, received):
    return total + received[...].astype(F32)


def plus_tailed(total, received):
    main = total[:-TAIL] + received[:-TAIL, :].astype(F32)
    tail = received[-TAIL:, :].astype(F32)
    more = tail[: TAIL // 2] + tail[TAIL // 2 :]
    return jnp.concatenate([main, total[-TAIL:] + jnp.concatenate([more, more], axis=0)], axis=0)


def split(value):
    high = value.astype(BF16).astype(F32)
    return high, value - high


def packed(total):
    high, low = split(total[-TAIL // 2 :])
    return jnp.concatenate([total[:-TAIL], high, low], axis=0).astype(BF16)


def place(dz):
    return (lax.axis_index("rep") + dz) & (NZ - 1)


def x_place():
    return lax.axis_index("rep") >> 3


def x_rows(panel_ref, which):
    at = pl.multiple_of(which * PART, PART)
    return jnp.concatenate([panel_ref[pl.ds(at, PART), :], panel_ref[HALF:, :]], axis=0)


def z_first_kernel(rows_ref, panel_ref, down, up):
    total = product(panel_ref[:HALF, :], rows_ref[place(NZ // 2)]).astype(BF16)
    down[...] = total[: HALF // 2]
    up[...] = total[HALF // 2 :]


def z_first(rows, panel, after):
    return call(
        z_first_kernel,
        [jax.ShapeDtypeStruct((HALF // 2, PAIR), BF16)] * 2,
        (rows, panel),
        after,
    )


def z_kernel(steps, rows_ref, panel_ref, *refs):
    received, outs = refs[: -len(steps)], refs[-len(steps) :]
    left = panel_ref[:HALF, :]
    for i, dz in enumerate(steps):
        total = product(left, rows_ref[place(dz)])
        count = received[i].shape[0]
        if count == HALF:
            total = plus(total, received[i])
        elif dz < 0:
            total = jnp.concatenate([plus(total[:count], received[i]), total[count:]], axis=0)
        else:
            total = jnp.concatenate([total[:-count], plus(total[-count:], received[i])], axis=0)
        outs[i][...] = total.astype(BF16)


def z_step(rows, panel, steps, received, after):
    return call(
        functools.partial(z_kernel, steps),
        [jax.ShapeDtypeStruct((HALF, PAIR), BF16)] * len(steps),
        (rows, panel, *received),
        after,
    )


def over_kernel(steps, rows_ref, panel_ref, out_ref):
    left = x_rows(panel_ref, 1 - x_place())
    for i, dz in enumerate(steps):
        out_ref[i] = packed(product(left, rows_ref[place(dz)]))


def over_x(rows, panel, steps, after):
    return call(
        functools.partial(over_kernel, steps),
        [jax.ShapeDtypeStruct((len(steps), PART + TAIL, PAIR), BF16)],
        (rows, panel),
        after,
    )


def x_kernel(steps, picks, n_over, rows_ref, panel_ref, *refs):
    over, refs = refs[:n_over], refs[n_over:]
    received, outs = refs[: -len(steps)], refs[-len(steps) :]
    left = x_rows(panel_ref, x_place())
    for i, dz in enumerate(steps):
        total = product(left, rows_ref[place(dz)])
        which, at = picks[i]
        total = plus_tailed(total, over[which].at[at])
        if i < len(received):
            total = plus_tailed(total, received[i])
        outs[i][...] = packed(total)


def x_step(rows, panel, steps, over, received, after):
    arrays, picks = [], []
    for dz in steps:
        array, at = over[dz]
        known = [a is array for a in arrays]
        if not any(known):
            known.append(True)
            arrays.append(array)
        picks.append((known.index(True), at))
    return call(
        functools.partial(x_kernel, steps, tuple(picks), len(arrays)),
        [jax.ShapeDtypeStruct((PART + TAIL, PAIR), BF16)] * len(steps),
        (rows, panel, *arrays, *received),
        after,
    )


def halves(total):
    cols = total.shape[0]
    return [
        jnp.concatenate([total[c : c + 64] for c in range(first, cols, 128)], axis=0).T
        for first in (0, 64)
    ]


def last_kernel(
    at, rows_ref, near_ref, other_ref, over, x_up, x_down, z_down, z_up,
    own_x, own_z, rhs, beside, cross, across, x_this, x_that, z_this, z_that,
):
    side = x_place()
    right = rows_ref[place(0)]
    total = product(x_rows(near_ref, side), right)
    total = plus_tailed(plus_tailed(plus_tailed(total, over.at[at]), x_up), x_down)
    x_this[...], x_that[...] = halves(total[:PART])
    tail = total[PART:]
    total = plus(plus(product(other_ref[:HALF, :], right), z_down), z_up)
    z_this[...], z_that[...] = halves(total)
    mine = pl.ds(pl.multiple_of(side * ROWS, ROWS), ROWS)
    theirs = pl.ds(pl.multiple_of((1 - side) * ROWS, ROWS), ROWS)
    own_x[...] = x_this[mine, :]
    own_z[...] = z_this[mine, :]
    for out, x, z, where in (
        (beside, x_this, z_this, theirs),
        (cross, x_that, z_that, theirs),
        (across, x_that, z_that, mine),
    ):
        high, low = split(x[where, :])
        out[:ROWS, :] = jnp.concatenate([high, low, z[where, :]], axis=1).astype(BF16)
    lower, upper = tail[: TAIL // 2, :ROWS], tail[: TAIL // 2, ROWS:]
    rhs[...] = jnp.where(side == 0, lower, upper)
    high, low = split(jnp.where(side == 0, upper, lower))
    sent = jnp.concatenate([high, low], axis=0)
    zeros = jnp.zeros((TAIL, HALF - ROWS), F32)
    cross[ROWS:, :] = jnp.concatenate([sent, zeros], axis=1).astype(BF16)


def last(rows, near, other, over, x_got, z_got, after):
    array, at = over
    message = jax.ShapeDtypeStruct((ROWS, HALF), BF16)
    return call(
        functools.partial(last_kernel, at),
        [
            jax.ShapeDtypeStruct((ROWS, PART // 2), F32),
            jax.ShapeDtypeStruct((ROWS, PART), F32),
            jax.ShapeDtypeStruct((TAIL // 2, ROWS), F32),
            message,
            jax.ShapeDtypeStruct((ROWS + TAIL, HALF), BF16),
            message,
        ],
        (rows, near, other, array, *x_got, *z_got),
        after,
        scratch=[pltpu.VMEM((PAIR, n), F32) for n in (PART // 2, PART // 2, PART, PART)],
    )


def parts(message_ref):
    value = message_ref[:ROWS, :].astype(F32)
    quarter = HALF // 4
    return value[:, :quarter] + value[:, quarter : 2 * quarter], value[:, 2 * quarter :]


def finish_kernel(
    own_x, own_z, rhs_ref, beside_ref, cross_ref, across_ref, out_ref, rhs_out
):
    side, row, half = x_place(), lax.axis_index("row"), lax.axis_index("col")
    y, core = row >> 1, row & 1
    (beside_x, beside_z), (cross_x, cross_z), (across_x, across_z) = (
        parts(r) for r in (beside_ref, cross_ref, across_ref)
    )
    for where_to, here, there, other in (
        (half, own_x[...], beside_x, own_z[...] + beside_z),
        (1 - half, across_x, cross_x, cross_z + across_z),
    ):
        near = jnp.concatenate(
            [jnp.where(side == 0, here, there), jnp.where(side == 0, there, here)], axis=1
        )
        first = jnp.where(core == 0, near, other)
        second = jnp.where(core == 0, other, near)
        for dy in range(4):
            lanes = slice(dy * 64, dy * 64 + 64)
            at = pl.multiple_of(((y + dy) & 3) * 128, 128)
            out_ref[0, where_to, :, pl.ds(at, 128)] = jnp.concatenate(
                [first[:, lanes], second[:, lanes]], axis=1
            )
    tail = cross_ref[ROWS:, :].astype(F32)[:, :ROWS]
    mine = rhs_ref[...][:1]
    other = (tail[: TAIL // 2] + tail[TAIL // 2 :])[:1]
    rhs_out[0] = jnp.concatenate(
        [jnp.where(half == 0, mine, other), jnp.where(half == 0, other, mine)], axis=0
    )


def finish(*args):
    return call(
        finish_kernel,
        [
            jax.ShapeDtypeStruct((1, 2, ROWS, HALF), F32),
            jax.ShapeDtypeStruct((1, 2, ROWS), F32),
        ],
        args,
    )


def z_shift(x, d):
    return lax.ppermute(
        x, "rep", [(a * NZ + z, a * NZ + (z + d) % NZ) for a in range(2) for z in range(NZ)]
    )


def x_swap(x):
    return lax.ppermute(
        x, "rep", [(a * NZ + z, (1 - a) * NZ + z) for a in range(2) for z in range(NZ)]
    )


def y_shift(x, d):
    return lax.ppermute(
        x, "row", [(y * 2 + c, (y + d) % 4 * 2 + c) for y in range(4) for c in range(2)]
    )


def core_swap(x):
    return lax.ppermute(x, "row", [(i, i ^ 1) for i in range(8)])


def half_swap(x):
    return lax.ppermute(x, "col", [(0, 1), (1, 0)])


def cross_swap(x):
    pairs = []
    for a in range(2):
        for z in range(NZ):
            for h in range(2):
                pairs.append(((a * NZ + z) * 2 + h, ((1 - a) * NZ + z) * 2 + 1 - h))
    return lax.ppermute(x, ("rep", "col"), pairs)


def per_device(design_rows, design_panel, observations, group_ids, group_sigma):
    points = design_rows.shape[0]
    mine = jnp.transpose(design_panel.reshape(points, -1))
    weights, weighted_obs = weigh(observations, group_ids, group_sigma)
    rows = pair_up(design_rows)

    foreign = half_swap(mine)
    blocks = [mine, foreign]
    for d in (1, 2, 3):
        blocks.append(y_shift(mine, -d))
    for d in (1, 2, 3):
        blocks.append(y_shift(foreign, -d))
    blocks = [blocks[i] for i in (0, 1, 2, 5, 3, 6, 4, 7)]
    near = collect(weights, weighted_obs, blocks, (rows,))
    other = core_swap(near)

    over, z_got, x_got, after = {}, (), (), ()

    def piece(*steps):
        nonlocal after
        (sent,) = over_x(rows, near, steps, after)
        after = (sent,)
        got = x_swap(sent)
        for i, dz in enumerate(steps):
            over[dz] = (got, i)

    def z_next(s):
        nonlocal after, z_got
        if s == NZ // 2:
            sent = z_first(rows, other, after)
        else:
            sent = z_step(rows, other, (-s, s), z_got, after)
        after = (sent[0],)
        z_got = (z_shift(sent[0], -1), z_shift(sent[1], 1))

    def x_next(s):
        nonlocal after, x_got
        steps = (s,) if s == 4 else (s, -s)
        sent = x_step(rows, near, steps, over, x_got, after)
        after = (sent[0],)
        x_got = (z_shift(sent[0], 1),) + tuple(z_shift(v, -1) for v in sent[1:])

    piece(4)
    piece(3, -3)
    z_next(4)
    x_next(4)
    z_next(3)
    piece(2, -2)
    x_next(3)
    piece(1, -1, 0)
    z_next(2)
    x_next(2)
    z_next(1)
    x_next(1)
    own_x, own_z, rhs_own, beside, cross, across = last(
        rows, near, other, over[0], x_got, z_got, after
    )
    return finish(
        own_x, own_z, rhs_own, x_swap(beside), cross_swap(cross), half_swap(across)
    )


def solution(mesh):
    in_specs = (P("rep", ("row", "col")), P("rep", "col", "row"), P("rep"), P("rep"), P())
    out_specs = (P("row", None, "rep", "col"), P("row", None, "rep"))
    return jax.shard_map(
        per_device, mesh=mesh, in_specs=in_specs, out_specs=out_specs, check_vma=False
    )
```

```python
import functools

import jax
import jax.numpy as jnp
from jax import lax
from jax.experimental import pallas as pl
from jax.experimental.pallas import tpu as pltpu
from jax.sharding import PartitionSpec as P

NZ = 8
ROWS = 192
PAIR = 2 * ROWS
HALF = 512
PART = 256
TAIL = 16
BF16, F32 = jnp.bfloat16, jnp.float32
IN_VMEM = pl.BlockSpec(memory_space=pltpu.VMEM)
IN_SMEM = pl.BlockSpec(memory_space=pltpu.SMEM)


def call(kernel, out_shape, args, after=(), scratch=(), cost=4e9):
    n, extra = len(args), len(after)

    def body(*refs):
        kernel(*refs[:n], *refs[n + extra :])

    return pl.pallas_call(
        body,
        out_shape=out_shape,
        in_specs=[IN_VMEM] * (n + extra),
        out_specs=[IN_VMEM] * len(out_shape),
        scratch_shapes=list(scratch),
        compiler_params=pltpu.CompilerParams(vmem_limit_bytes=16 * 2**20),
        cost_estimate=pl.CostEstimate(flops=int(cost), bytes_accessed=1, transcendentals=0),
    )(*args, *after)


def weigh_kernel(sigma_ref, obs_ref, ids_ref, weights_out, obs_out):
    ids = ids_ref[...]
    sigma = jnp.full(ids.shape, sigma_ref[0], F32)
    for g in range(1, sigma_ref.shape[0]):
        sigma = jnp.where(ids == g, sigma_ref[g], sigma)
    weights = 1.0 / (sigma * sigma)
    weights_out[...] = jnp.broadcast_to(weights, weights_out.shape)
    weighted = (weights * obs_ref[...]).astype(BF16)
    obs_out[...] = jnp.broadcast_to(weighted, obs_out.shape)


def weigh(observations, group_ids, group_sigma):
    points = observations.shape[0]
    flat = pl.BlockSpec((1, points), lambda i: (0, 0))
    return pl.pallas_call(
        weigh_kernel,
        grid=(1,),
        out_shape=(
            jax.ShapeDtypeStruct((8, points), F32),
            jax.ShapeDtypeStruct((TAIL, points), BF16),
        ),
        in_specs=[IN_SMEM, flat, flat],
        out_specs=[IN_VMEM, IN_VMEM],
        compiler_params=pltpu.CompilerParams(vmem_limit_bytes=2 * 2**20),
    )(group_sigma, observations.reshape(1, -1), group_ids.reshape(1, -1))


def pair_kernel(first_ref, second_ref, out_ref):
    e = pl.program_id(0)
    for half in range(2):
        lanes = slice(half * ROWS, (half + 1) * ROWS)
        out_ref[2 * e + half] = jnp.concatenate(
            [first_ref[:, lanes], second_ref[:, lanes]], axis=1
        )


def pair_up(design_rows):
    points = design_rows.shape[0]
    return pl.pallas_call(
        pair_kernel,
        grid=(NZ // 2,),
        out_shape=jax.ShapeDtypeStruct((NZ, points, PAIR), BF16),
        in_specs=[
            pl.BlockSpec((points, PAIR), lambda e: (0, e)),
            pl.BlockSpec((points, PAIR), lambda e: (0, e + NZ // 2)),
        ],
        out_specs=IN_VMEM,
        compiler_params=pltpu.CompilerParams(vmem_limit_bytes=12 * 2**20),
        cost_estimate=pl.CostEstimate(
            flops=0, bytes_accessed=4 * design_rows.size, transcendentals=0
        ),
    )(design_rows, design_rows)


def collect_kernel(weights_ref, obs_ref, *refs):
    weights = weights_ref[:1, :]
    out, at = refs[-1], 0
    for ref in refs[:-1]:
        value = weights * ref[...].astype(F32)
        out[at : at + ref.shape[0], :] = value.astype(BF16)
        at += ref.shape[0]
    out[at:, :] = obs_ref[...]


def collect(weights, weighted_obs, blocks, after):
    rows = sum(b.shape[0] for b in blocks) + weighted_obs.shape[0]
    return call(
        collect_kernel,
        [jax.ShapeDtypeStruct((rows, weights.shape[1]), BF16)],
        (weights, weighted_obs, *blocks),
        after,
        cost=1e9,
    )[0]


def product(left, right):
    return jnp.dot(left, right, preferred_element_type=F32)


def plus(total, received):
    return total + received[...].astype(F32)


def plus_tailed(total, received):
    main = total[:-TAIL] + received[:-TAIL, :].astype(F32)
    tail = received[-TAIL:, :].astype(F32)
    more = tail[: TAIL // 2] + tail[TAIL // 2 :]
    return jnp.concatenate([main, total[-TAIL:] + jnp.concatenate([more, more], axis=0)], axis=0)


def split(value):
    high = value.astype(BF16).astype(F32)
    return high, value - high


def packed(total):
    high, low = split(total[-TAIL // 2 :])
    return jnp.concatenate([total[:-TAIL], high, low], axis=0).astype(BF16)


def place(dz):
    return (lax.axis_index("rep") + dz) & (NZ - 1)


def x_place():
    return lax.axis_index("rep") >> 3


def x_rows(panel_ref, which):
    at = pl.multiple_of(which * PART, PART)
    return jnp.concatenate([panel_ref[pl.ds(at, PART), :], panel_ref[HALF:, :]], axis=0)


def z_first_kernel(rows_ref, panel_ref, down, up):
    total = product(panel_ref[:HALF, :], rows_ref[place(NZ // 2)]).astype(BF16)
    down[...] = total[: HALF // 2]
    up[...] = total[HALF // 2 :]


def z_first(rows, panel, after):
    return call(
        z_first_kernel,
        [jax.ShapeDtypeStruct((HALF // 2, PAIR), BF16)] * 2,
        (rows, panel),
        after,
        cost=3000000000.0,
    )


def z_product_kernel(steps, rows_ref, panel_ref, *outs):
    left = panel_ref[:HALF, :]
    for out, dz in zip(outs, steps):
        out[...] = product(left, rows_ref[place(dz)])


def z_product(rows, panel, steps, after):
    return call(
        functools.partial(z_product_kernel, steps),
        [jax.ShapeDtypeStruct((HALF, PAIR), F32)] * len(steps),
        (rows, panel),
        after,
        cost=1000000000.0,
    )


def z_add_kernel(*refs):
    n = len(refs) // 3
    for i, (ready, received, out) in enumerate(zip(refs[:n], refs[n : 2 * n], refs[2 * n :])):
        count = received.shape[0]
        if count == HALF:
            out[...] = plus(ready[...], received).astype(BF16)
            continue
        low = slice(0, count) if i == 0 else slice(HALF - count, HALF)
        rest = slice(count, HALF) if i == 0 else slice(0, HALF - count)
        out[low, :] = plus(ready[low, :], received).astype(BF16)
        out[rest, :] = ready[rest, :].astype(BF16)


def z_step(ready, received, after):
    return call(
        z_add_kernel,
        [jax.ShapeDtypeStruct((HALF, PAIR), BF16)] * 2,
        (*ready, *received),
        after,
        cost=3000000000.0,
    )


def over_kernel(steps, rows_ref, panel_ref, out_ref):
    left = x_rows(panel_ref, 1 - x_place())
    for i, dz in enumerate(steps):
        out_ref[i] = packed(product(left, rows_ref[place(dz)]))


def over_x(rows, panel, steps, after):
    return call(
        functools.partial(over_kernel, steps),
        [jax.ShapeDtypeStruct((len(steps), PART + TAIL, PAIR), BF16)],
        (rows, panel),
        after,
        cost=2000000000.0,
    )


def x_kernel(steps, picks, n_over, rows_ref, panel_ref, *refs):
    over, refs = refs[:n_over], refs[n_over:]
    received, outs = refs[: -len(steps)], refs[-len(steps) :]
    left = x_rows(panel_ref, x_place())
    for i, dz in enumerate(steps):
        total = product(left, rows_ref[place(dz)])
        which, at = picks[i]
        total = plus_tailed(total, over[which].at[at])
        if i < len(received):
            total = plus_tailed(total, received[i])
        outs[i][...] = packed(total)


def x_step(rows, panel, steps, over, received, after):
    arrays, picks = [], []
    for dz in steps:
        array, at = over[dz]
        known = [a is array for a in arrays]
        if not any(known):
            known.append(True)
            arrays.append(array)
        picks.append((known.index(True), at))
    return call(
        functools.partial(x_kernel, steps, tuple(picks), len(arrays)),
        [jax.ShapeDtypeStruct((PART + TAIL, PAIR), BF16)] * len(steps),
        (rows, panel, *arrays, *received),
        after,
        cost=3000000000.0,
    )


def halves(total):
    cols = total.shape[0]
    return [
        jnp.concatenate([total[c : c + 64] for c in range(first, cols, 128)], axis=0).T
        for first in (0, 64)
    ]


def own_and_theirs():
    side = x_place()
    return (
        pl.ds(pl.multiple_of(side * ROWS, ROWS), ROWS),
        pl.ds(pl.multiple_of((1 - side) * ROWS, ROWS), ROWS),
    )


def ahead_kernel(at, rows_ref, near_ref, other_ref, over, ready_x, ready_z):
    right = rows_ref[place(0)]
    ready_x[...] = plus_tailed(product(x_rows(near_ref, x_place()), right), over.at[at])
    ready_z[...] = product(other_ref[:HALF, :], right)


def last_ahead(rows, near, other, over, after):
    array, at = over
    return call(
        functools.partial(ahead_kernel, at),
        [
            jax.ShapeDtypeStruct((PART + TAIL, PAIR), F32),
            jax.ShapeDtypeStruct((HALF, PAIR), F32),
        ],
        (rows, near, other, array),
        after,
        cost=1e9,
    )


def z_last_kernel(ready, z_down, z_up, own, beside, cross, across, this, that):
    this[...], that[...] = halves(plus(plus(ready[...], z_down), z_up))
    mine, theirs = own_and_theirs()
    own[...] = this[mine, :]
    beside[...] = this[theirs, :].astype(BF16)
    cross[...] = that[theirs, :].astype(BF16)
    across[...] = that[mine, :].astype(BF16)


def z_last(ready, z_got):
    message = jax.ShapeDtypeStruct((ROWS, PART), BF16)
    return call(
        z_last_kernel,
        [jax.ShapeDtypeStruct((ROWS, PART), F32), message, message, message],
        (ready, *z_got),
        scratch=[pltpu.VMEM((PAIR, PART), F32)] * 2,
        cost=3e9,
    )


def x_last_kernel(ready, z_beside, up, down, own, rhs, beside, cross, across, this, that):
    side = x_place()
    total = plus_tailed(plus_tailed(ready[...], up), down)
    this[...], that[...] = halves(total[:PART])
    mine, theirs = own_and_theirs()
    own[...] = this[mine, :]
    for out, value in (
        (beside, this[theirs, :]),
        (cross, that[theirs, :]),
        (across, that[mine, :]),
    ):
        out[:ROWS, :PART] = jnp.concatenate(split(value), axis=1).astype(BF16)
    beside[:, PART:] = z_beside[...]
    tail = total[PART:]
    lower, upper = tail[: TAIL // 2, :ROWS], tail[: TAIL // 2, ROWS:]
    rhs[...] = jnp.where(side == 0, lower, upper)
    sent = jnp.concatenate(split(jnp.where(side == 0, upper, lower)), axis=0)
    zeros = jnp.zeros((TAIL, PART - ROWS), F32)
    cross[ROWS:, :] = jnp.concatenate([sent, zeros], axis=1).astype(BF16)


def x_last(ready, z_beside, x_got, after):
    return call(
        x_last_kernel,
        [
            jax.ShapeDtypeStruct((ROWS, PART // 2), F32),
            jax.ShapeDtypeStruct((TAIL // 2, ROWS), F32),
            jax.ShapeDtypeStruct((ROWS, HALF), BF16),
            jax.ShapeDtypeStruct((ROWS + TAIL, PART), BF16),
            jax.ShapeDtypeStruct((ROWS, PART), BF16),
        ],
        (ready, z_beside, *x_got),
        after,
        cost=8e9,
        scratch=[pltpu.VMEM((PAIR, PART // 2), F32)] * 2,
    )


def foreign_kernel(first, second, out):
    out[...] = plus(first[...].astype(F32), second)


def foreign_z(first, second, after):
    return call(
        foreign_kernel,
        [jax.ShapeDtypeStruct(first.shape, F32)],
        (first, second),
        after,
        cost=3e9,
    )[0]


def whole(message_ref):
    value = message_ref[:ROWS, :PART].astype(F32)
    return value[:, : PART // 2] + value[:, PART // 2 :]


def finish_kernel(
    own_x, own_z, rhs_ref, there_z, beside, cross, across, out_ref, rhs_out
):
    side, row, half = x_place(), lax.axis_index("row"), lax.axis_index("col")
    y, core = row >> 1, row & 1
    beside_z = beside[:, PART:].astype(F32)
    for where_to, here, there, other in (
        (half, own_x[...], whole(beside), own_z[...] + beside_z),
        (1 - half, whole(across), whole(cross), there_z[...]),
    ):
        near = jnp.concatenate(
            [jnp.where(side == 0, here, there), jnp.where(side == 0, there, here)], axis=1
        )
        first = jnp.where(core == 0, near, other)
        second = jnp.where(core == 0, other, near)
        for dy in range(4):
            lanes = slice(dy * 64, dy * 64 + 64)
            at = pl.multiple_of(((y + dy) & 3) * 128, 128)
            out_ref[0, where_to, :, pl.ds(at, 128)] = jnp.concatenate(
                [first[:, lanes], second[:, lanes]], axis=1
            )
    tail = cross[ROWS:, :].astype(F32)[:, :ROWS]
    mine = rhs_ref[...][:1]
    other = (tail[: TAIL // 2] + tail[TAIL // 2 :])[:1]
    rhs_out[0] = jnp.concatenate(
        [jnp.where(half == 0, mine, other), jnp.where(half == 0, other, mine)], axis=0
    )


def finish(*args):
    return call(
        finish_kernel,
        [
            jax.ShapeDtypeStruct((1, 2, ROWS, HALF), F32),
            jax.ShapeDtypeStruct((1, 2, ROWS), F32),
        ],
        args,
    )


def z_shift(x, d):
    return lax.ppermute(
        x, "rep", [(a * NZ + z, a * NZ + (z + d) % NZ) for a in range(2) for z in range(NZ)]
    )


def x_swap(x):
    return lax.ppermute(
        x, "rep", [(a * NZ + z, (1 - a) * NZ + z) for a in range(2) for z in range(NZ)]
    )


def y_shift(x, d):
    return lax.ppermute(
        x, "row", [(y * 2 + c, (y + d) % 4 * 2 + c) for y in range(4) for c in range(2)]
    )


def core_swap(x):
    return lax.ppermute(x, "row", [(i, i ^ 1) for i in range(8)])


def half_swap(x):
    return lax.ppermute(x, "col", [(0, 1), (1, 0)])


def cross_swap(x):
    pairs = []
    for a in range(2):
        for z in range(NZ):
            for h in range(2):
                pairs.append(((a * NZ + z) * 2 + h, ((1 - a) * NZ + z) * 2 + 1 - h))
    return lax.ppermute(x, ("rep", "col"), pairs)


def per_device(design_rows, design_panel, observations, group_ids, group_sigma):
    points = design_rows.shape[0]
    mine = jnp.transpose(design_panel.reshape(points, -1))
    weights, weighted_obs = weigh(observations, group_ids, group_sigma)
    rows = pair_up(design_rows)

    foreign = half_swap(mine)
    blocks = [mine, foreign]
    for d in (1, 2, 3):
        blocks.append(y_shift(mine, -d))
    for d in (1, 2, 3):
        blocks.append(y_shift(foreign, -d))
    blocks = [blocks[i] for i in (0, 1, 2, 5, 3, 6, 4, 7)]
    near = collect(weights, weighted_obs, blocks, (rows,))
    other = core_swap(near)

    over, z_got, x_got, ready, after = {}, (), (), (), ()

    def piece(*steps):
        nonlocal after
        (sent,) = over_x(rows, near, steps, after)
        after = (sent,)
        got = x_swap(sent)
        for i, dz in enumerate(steps):
            over[dz] = (got, i)

    def z_ahead(s):
        nonlocal after, ready
        ready = z_product(rows, other, (-s, s), after)
        after = (ready[0],)

    def z_next(s):
        nonlocal after, z_got
        if s == NZ // 2:
            sent = z_first(rows, other, after)
        else:
            sent = z_step(ready, z_got, after)
        after = (sent[0],)
        z_got = (z_shift(sent[0], -1), z_shift(sent[1], 1))

    def x_next(s):
        nonlocal after, x_got
        steps = (s,) if s == 4 else (s, -s)
        sent = x_step(rows, near, steps, over, x_got, after)
        after = (sent[0],)
        x_got = (z_shift(sent[0], 1),) + tuple(z_shift(v, -1) for v in sent[1:])

    piece(4)
    piece(3, -3)
    z_next(4)
    x_next(4)
    z_ahead(3)
    z_next(3)
    piece(2, -2)
    x_next(3)
    piece(1, -1, 0)
    z_ahead(2)
    z_next(2)
    x_next(2)
    z_ahead(1)
    z_next(1)
    x_next(1)
    ready_x, ready_z = last_ahead(rows, near, other, over[0], after)
    own_z, beside_z, cross_z, across_z = z_last(ready_z, z_got)
    across_z, cross_z = half_swap(across_z), cross_swap(cross_z)
    own_x, rhs_own, beside, cross, across = x_last(ready_x, beside_z, x_got, (own_z,))
    there_z = foreign_z(cross_z, across_z, (own_x,))
    return finish(
        own_x, own_z, rhs_own, there_z, x_swap(beside), cross_swap(cross), half_swap(across)
    )


def solution(mesh):
    in_specs = (P("rep", ("row", "col")), P("rep", "col", "row"), P("rep"), P("rep"), P())
    out_specs = (P("row", None, "rep", "col"), P("row", None, "rep"))
    return jax.shard_map(
        per_device, mesh=mesh, in_specs=in_specs, out_specs=out_specs, check_vma=False
    )
```

```python
import functools

import jax
import jax.numpy as jnp
from jax import lax
from jax.experimental import pallas as pl
from jax.experimental.pallas import tpu as pltpu
from jax.sharding import PartitionSpec as P

NZ = 8
ROWS = 192
PAIR = 2 * ROWS
HALF = 512
PART = 256
TAIL = 16
BF16, F32 = jnp.bfloat16, jnp.float32
IN_VMEM = pl.BlockSpec(memory_space=pltpu.VMEM)
IN_SMEM = pl.BlockSpec(memory_space=pltpu.SMEM)


def call(kernel, out_shape, args, after=(), scratch=(), cost=4e9):
    n, extra = len(args), len(after)

    def body(*refs):
        kernel(*refs[:n], *refs[n + extra :])

    return pl.pallas_call(
        body,
        out_shape=out_shape,
        in_specs=[IN_VMEM] * (n + extra),
        out_specs=[IN_VMEM] * len(out_shape),
        scratch_shapes=list(scratch),
        compiler_params=pltpu.CompilerParams(vmem_limit_bytes=16 * 2**20),
        cost_estimate=pl.CostEstimate(flops=int(cost), bytes_accessed=1, transcendentals=0),
    )(*args, *after)


def weigh_kernel(sigma_ref, obs_ref, ids_ref, weights_out, obs_out):
    ids = ids_ref[...]
    sigma = jnp.full(ids.shape, sigma_ref[0], F32)
    for g in range(1, sigma_ref.shape[0]):
        sigma = jnp.where(ids == g, sigma_ref[g], sigma)
    weights = 1.0 / (sigma * sigma)
    weights_out[...] = jnp.broadcast_to(weights, weights_out.shape)
    weighted = (weights * obs_ref[...]).astype(BF16)
    obs_out[...] = jnp.broadcast_to(weighted, obs_out.shape)


def weigh(observations, group_ids, group_sigma):
    points = observations.shape[0]
    flat = pl.BlockSpec((1, points), lambda i: (0, 0))
    return pl.pallas_call(
        weigh_kernel,
        grid=(1,),
        out_shape=(
            jax.ShapeDtypeStruct((8, points), F32),
            jax.ShapeDtypeStruct((TAIL, points), BF16),
        ),
        in_specs=[IN_SMEM, flat, flat],
        out_specs=[IN_VMEM, IN_VMEM],
        compiler_params=pltpu.CompilerParams(vmem_limit_bytes=2 * 2**20),
    )(group_sigma, observations.reshape(1, -1), group_ids.reshape(1, -1))


def pair_kernel(first_ref, second_ref, out_ref):
    e = pl.program_id(0)
    for half in range(2):
        lanes = slice(half * ROWS, (half + 1) * ROWS)
        out_ref[2 * e + half] = jnp.concatenate(
            [first_ref[:, lanes], second_ref[:, lanes]], axis=1
        )


def pair_up(design_rows):
    points = design_rows.shape[0]
    return pl.pallas_call(
        pair_kernel,
        grid=(NZ // 2,),
        out_shape=jax.ShapeDtypeStruct((NZ, points, PAIR), BF16),
        in_specs=[
            pl.BlockSpec((points, PAIR), lambda e: (0, e)),
            pl.BlockSpec((points, PAIR), lambda e: (0, e + NZ // 2)),
        ],
        out_specs=IN_VMEM,
        compiler_params=pltpu.CompilerParams(vmem_limit_bytes=12 * 2**20),
        cost_estimate=pl.CostEstimate(
            flops=0, bytes_accessed=4 * design_rows.size, transcendentals=0
        ),
    )(design_rows, design_rows)


def collect_kernel(weights_ref, obs_ref, *refs):
    weights = weights_ref[:1, :]
    out, at = refs[-1], 0
    for ref in refs[:-1]:
        value = weights * ref[...].astype(F32)
        out[at : at + ref.shape[0], :] = value.astype(BF16)
        at += ref.shape[0]
    out[at:, :] = obs_ref[...]


def collect(weights, weighted_obs, blocks, after):
    rows = sum(b.shape[0] for b in blocks) + weighted_obs.shape[0]
    return call(
        collect_kernel,
        [jax.ShapeDtypeStruct((rows, weights.shape[1]), BF16)],
        (weights, weighted_obs, *blocks),
        after,
        cost=1e9,
    )[0]


def product(left, right):
    return jnp.dot(left, right, preferred_element_type=F32)


def plus(total, received):
    return total + received[...].astype(F32)


def plus_tailed(total, received):
    main = total[:-TAIL] + received[:-TAIL, :].astype(F32)
    tail = received[-TAIL:, :].astype(F32)
    more = tail[: TAIL // 2] + tail[TAIL // 2 :]
    return jnp.concatenate([main, total[-TAIL:] + jnp.concatenate([more, more], axis=0)], axis=0)


def split(value):
    high = value.astype(BF16).astype(F32)
    return high, value - high


def packed(total):
    high, low = split(total[-TAIL // 2 :])
    return jnp.concatenate([total[:-TAIL], high, low], axis=0).astype(BF16)


def place(dz):
    return (lax.axis_index("rep") + dz) & (NZ - 1)


def x_place():
    return lax.axis_index("rep") >> 3


def x_rows(panel_ref, which):
    at = pl.multiple_of(which * PART, PART)
    return jnp.concatenate([panel_ref[pl.ds(at, PART), :], panel_ref[HALF:, :]], axis=0)


def z_first_kernel(rows_ref, panel_ref, down, up):
    total = product(panel_ref[:HALF, :], rows_ref[place(NZ // 2)]).astype(BF16)
    down[...] = total[: HALF // 2]
    up[...] = total[HALF // 2 :]


def z_first(rows, panel, after):
    return call(
        z_first_kernel,
        [jax.ShapeDtypeStruct((HALF // 2, PAIR), BF16)] * 2,
        (rows, panel),
        after,
        cost=3000000000.0,
    )


def z_product_kernel(steps, rows_ref, panel_ref, *outs):
    left = panel_ref[:HALF, :]
    for out, dz in zip(outs, steps):
        out[...] = product(left, rows_ref[place(dz)])


def z_product(rows, panel, steps, after):
    return call(
        functools.partial(z_product_kernel, steps),
        [jax.ShapeDtypeStruct((HALF, PAIR), F32)] * len(steps),
        (rows, panel),
        after,
        cost=1000000000.0,
    )


def z_add_kernel(*refs):
    n = len(refs) // 3
    for i, (ready, received, out) in enumerate(zip(refs[:n], refs[n : 2 * n], refs[2 * n :])):
        count = received.shape[0]
        if count == HALF:
            out[...] = plus(ready[...], received).astype(BF16)
            continue
        low = slice(0, count) if i == 0 else slice(HALF - count, HALF)
        rest = slice(count, HALF) if i == 0 else slice(0, HALF - count)
        out[low, :] = plus(ready[low, :], received).astype(BF16)
        out[rest, :] = ready[rest, :].astype(BF16)


def z_step(ready, received, after):
    return call(
        z_add_kernel,
        [jax.ShapeDtypeStruct((HALF, PAIR), BF16)] * 2,
        (*ready, *received),
        after,
        cost=3000000000.0,
    )


def over_kernel(steps, rows_ref, panel_ref, out_ref):
    left = x_rows(panel_ref, 1 - x_place())
    for i, dz in enumerate(steps):
        out_ref[i] = packed(product(left, rows_ref[place(dz)]))


def over_x(rows, panel, steps, after):
    return call(
        functools.partial(over_kernel, steps),
        [jax.ShapeDtypeStruct((len(steps), PART + TAIL, PAIR), BF16)],
        (rows, panel),
        after,
        cost=2000000000.0,
    )


def x_kernel(steps, picks, n_over, rows_ref, panel_ref, *refs):
    over, refs = refs[:n_over], refs[n_over:]
    received, outs = refs[: -len(steps)], refs[-len(steps) :]
    left = x_rows(panel_ref, x_place())
    for i, dz in enumerate(steps):
        total = product(left, rows_ref[place(dz)])
        which, at = picks[i]
        total = plus_tailed(total, over[which].at[at])
        if i < len(received):
            total = plus_tailed(total, received[i])
        outs[i][...] = packed(total)


def x_step(rows, panel, steps, over, received, after):
    arrays, picks = [], []
    for dz in steps:
        array, at = over[dz]
        known = [a is array for a in arrays]
        if not any(known):
            known.append(True)
            arrays.append(array)
        picks.append((known.index(True), at))
    return call(
        functools.partial(x_kernel, steps, tuple(picks), len(arrays)),
        [jax.ShapeDtypeStruct((PART + TAIL, PAIR), BF16)] * len(steps),
        (rows, panel, *arrays, *received),
        after,
        cost=3000000000.0,
    )


def halves(total):
    cols = total.shape[0]
    return [
        jnp.concatenate([total[c : c + 64] for c in range(first, cols, 128)], axis=0).T
        for first in (0, 64)
    ]


def own_and_theirs():
    side = x_place()
    return (
        pl.ds(pl.multiple_of(side * ROWS, ROWS), ROWS),
        pl.ds(pl.multiple_of((1 - side) * ROWS, ROWS), ROWS),
    )


def ahead_kernel(at, rows_ref, near_ref, other_ref, over, ready_x, ready_z):
    right = rows_ref[place(0)]
    ready_x[...] = plus_tailed(product(x_rows(near_ref, x_place()), right), over.at[at])
    ready_z[...] = product(other_ref[:HALF, :], right)


def last_ahead(rows, near, other, over, after):
    array, at = over
    return call(
        functools.partial(ahead_kernel, at),
        [
            jax.ShapeDtypeStruct((PART + TAIL, PAIR), F32),
            jax.ShapeDtypeStruct((HALF, PAIR), F32),
        ],
        (rows, near, other, array),
        after,
        cost=1e9,
    )


def z_last_kernel(ready, z_down, z_up, own, beside, cross, across, this, that):
    this[...], that[...] = halves(plus(plus(ready[...], z_down), z_up))
    mine, theirs = own_and_theirs()
    own[...] = this[mine, :]
    beside[...] = this[theirs, :].astype(BF16)
    cross[...] = that[theirs, :].astype(BF16)
    across[...] = that[mine, :].astype(BF16)


def z_last(ready, z_got):
    message = jax.ShapeDtypeStruct((ROWS, PART), BF16)
    return call(
        z_last_kernel,
        [jax.ShapeDtypeStruct((ROWS, PART), F32), message, message, message],
        (ready, *z_got),
        scratch=[pltpu.VMEM((PAIR, PART), F32)] * 2,
        cost=3e9,
    )


def x_last_kernel(ready, z_beside, up, down, own, rhs, beside, cross, across, this, that):
    side = x_place()
    total = plus_tailed(plus_tailed(ready[...], up), down)
    this[...], that[...] = halves(total[:PART])
    mine, theirs = own_and_theirs()
    own[...] = this[mine, :]
    for out, value in (
        (beside, this[theirs, :]),
        (cross, that[theirs, :]),
        (across, that[mine, :]),
    ):
        out[:ROWS, :PART] = jnp.concatenate(split(value), axis=1).astype(BF16)
    beside[:, PART:] = z_beside[...]
    tail = total[PART:]
    lower, upper = tail[: TAIL // 2, :ROWS], tail[: TAIL // 2, ROWS:]
    rhs[...] = jnp.where(side == 0, lower, upper)
    sent = jnp.concatenate(split(jnp.where(side == 0, upper, lower)), axis=0)
    zeros = jnp.zeros((TAIL, PART - ROWS), F32)
    cross[ROWS:, :] = jnp.concatenate([sent, zeros], axis=1).astype(BF16)


def x_last(ready, z_beside, x_got, after):
    return call(
        x_last_kernel,
        [
            jax.ShapeDtypeStruct((ROWS, PART // 2), F32),
            jax.ShapeDtypeStruct((TAIL // 2, ROWS), F32),
            jax.ShapeDtypeStruct((ROWS, HALF), BF16),
            jax.ShapeDtypeStruct((ROWS + TAIL, PART), BF16),
            jax.ShapeDtypeStruct((ROWS, PART), BF16),
        ],
        (ready, z_beside, *x_got),
        after,
        cost=8e9,
        scratch=[pltpu.VMEM((PAIR, PART // 2), F32)] * 2,
    )


def foreign_kernel(first, second, out):
    out[...] = plus(first[...].astype(F32), second)


def foreign_z(first, second, after):
    return call(
        foreign_kernel,
        [jax.ShapeDtypeStruct(first.shape, F32)],
        (first, second),
        after,
        cost=3e9,
    )[0]


def whole(message_ref):
    value = message_ref[:ROWS, :PART].astype(F32)
    return value[:, : PART // 2] + value[:, PART // 2 :]


def finish_kernel(
    own_x, own_z, rhs_ref, there_z, beside, cross, across, out_ref, rhs_out
):
    side, row, half = x_place(), lax.axis_index("row"), lax.axis_index("col")
    y, core = row >> 1, row & 1
    beside_z = beside[:, PART:].astype(F32)
    for where_to, here, there, other in (
        (half, own_x[...], whole(beside), own_z[...] + beside_z),
        (1 - half, whole(across), whole(cross), there_z[...]),
    ):
        near = jnp.concatenate(
            [jnp.where(side == 0, here, there), jnp.where(side == 0, there, here)], axis=1
        )
        first = jnp.where(core == 0, near, other)
        second = jnp.where(core == 0, other, near)
        for dy in range(4):
            lanes = slice(dy * 64, dy * 64 + 64)
            at = pl.multiple_of(((y + dy) & 3) * 128, 128)
            out_ref[0, where_to, :, pl.ds(at, 128)] = jnp.concatenate(
                [first[:, lanes], second[:, lanes]], axis=1
            )
    tail = cross[ROWS:, :].astype(F32)[:, :ROWS]
    mine = rhs_ref[...][:1]
    other = (tail[: TAIL // 2] + tail[TAIL // 2 :])[:1]
    rhs_out[0] = jnp.concatenate(
        [jnp.where(half == 0, mine, other), jnp.where(half == 0, other, mine)], axis=0
    )


def finish(*args):
    return call(
        finish_kernel,
        [
            jax.ShapeDtypeStruct((1, 2, ROWS, HALF), F32),
            jax.ShapeDtypeStruct((1, 2, ROWS), F32),
        ],
        args,
    )


def z_shift(x, d):
    return lax.ppermute(
        x, "rep", [(a * NZ + z, a * NZ + (z + d) % NZ) for a in range(2) for z in range(NZ)]
    )


def x_swap(x):
    return lax.ppermute(
        x, "rep", [(a * NZ + z, (1 - a) * NZ + z) for a in range(2) for z in range(NZ)]
    )


def y_shift(x, d):
    return lax.ppermute(
        x, "row", [(y * 2 + c, (y + d) % 4 * 2 + c) for y in range(4) for c in range(2)]
    )


def core_swap(x):
    return lax.ppermute(x, "row", [(i, i ^ 1) for i in range(8)])


def half_swap(x):
    return lax.ppermute(x, "col", [(0, 1), (1, 0)])


def cross_swap(x):
    pairs = []
    for a in range(2):
        for z in range(NZ):
            for h in range(2):
                pairs.append(((a * NZ + z) * 2 + h, ((1 - a) * NZ + z) * 2 + 1 - h))
    return lax.ppermute(x, ("rep", "col"), pairs)


def per_device(design_rows, design_panel, observations, group_ids, group_sigma):
    points = design_rows.shape[0]
    mine = jnp.transpose(design_panel.reshape(points, -1))
    weights, weighted_obs = weigh(observations, group_ids, group_sigma)
    rows = pair_up(design_rows)

    foreign = half_swap(mine)
    blocks = [mine, foreign]
    for d in (1, 2, 3):
        blocks.append(y_shift(mine, -d))
    for d in (1, 2, 3):
        blocks.append(y_shift(foreign, -d))
    blocks = [blocks[i] for i in (0, 1, 2, 5, 3, 6, 4, 7)]
    near = collect(weights, weighted_obs, blocks, (rows,))
    other = core_swap(near)

    over, z_got, x_got, ready, after = {}, (), (), (), ()

    def piece(*steps):
        nonlocal after
        (sent,) = over_x(rows, near, steps, after)
        after = (sent,)
        got = x_swap(sent)
        for i, dz in enumerate(steps):
            over[dz] = (got, i)

    def z_ahead(s):
        nonlocal after, ready
        ready = z_product(rows, other, (-s, s), after)
        after = (ready[0],)

    def z_next(s):
        nonlocal after, z_got
        if s == NZ // 2:
            sent = z_first(rows, other, after)
        else:
            sent = z_step(ready, z_got, after)
        after = (sent[0],)
        z_got = (z_shift(sent[0], -1), z_shift(sent[1], 1))

    def x_next(s):
        nonlocal after, x_got
        steps = (s,) if s == 4 else (s, -s)
        sent = x_step(rows, near, steps, over, x_got, after)
        after = (sent[0],)
        x_got = (z_shift(sent[0], 1),) + tuple(z_shift(v, -1) for v in sent[1:])

    piece(4)
    z_next(4)
    piece(3, -3)
    x_next(4)
    z_ahead(3)
    z_next(3)
    x_next(3)
    piece(2, -2)
    z_ahead(2)
    z_next(2)
    piece(1, -1, 0)
    x_next(2)
    z_ahead(1)
    z_next(1)
    x_next(1)
    ready_x, ready_z = last_ahead(rows, near, other, over[0], after)
    own_z, beside_z, cross_z, across_z = z_last(ready_z, z_got)
    across_z, cross_z = half_swap(across_z), cross_swap(cross_z)
    own_x, rhs_own, beside, cross, across = x_last(ready_x, beside_z, x_got, (own_z,))
    there_z = foreign_z(cross_z, across_z, (own_x,))
    return finish(
        own_x, own_z, rhs_own, there_z, x_swap(beside), cross_swap(cross), half_swap(across)
    )


def solution(mesh):
    in_specs = (P("rep", ("row", "col")), P("rep", "col", "row"), P("rep"), P("rep"), P())
    out_specs = (P("row", None, "rep", "col"), P("row", None, "rep"))
    return jax.shard_map(
        per_device, mesh=mesh, in_specs=in_specs, out_specs=out_specs, check_vma=False
    )
```

```python
import functools

import jax
import jax.numpy as jnp
from jax import lax
from jax.experimental import pallas as pl
from jax.experimental.pallas import tpu as pltpu
from jax.sharding import PartitionSpec as P

NZ = 8
ROWS = 192
PAIR = 2 * ROWS
HALF = 512
PART = 256
TAIL = 16
BF16, F32 = jnp.bfloat16, jnp.float32
IN_VMEM = pl.BlockSpec(memory_space=pltpu.VMEM)
IN_SMEM = pl.BlockSpec(memory_space=pltpu.SMEM)


def call(kernel, out_shape, args, after=(), scratch=(), cost=4e9):
    n, extra = len(args), len(after)

    def body(*refs):
        kernel(*refs[:n], *refs[n + extra :])

    return pl.pallas_call(
        body,
        out_shape=out_shape,
        in_specs=[IN_VMEM] * (n + extra),
        out_specs=[IN_VMEM] * len(out_shape),
        scratch_shapes=list(scratch),
        compiler_params=pltpu.CompilerParams(vmem_limit_bytes=16 * 2**20),
        cost_estimate=pl.CostEstimate(flops=int(cost), bytes_accessed=1, transcendentals=0),
    )(*args, *after)


def weigh_kernel(sigma_ref, obs_ref, ids_ref, weights_out, obs_out):
    ids = ids_ref[...]
    sigma = jnp.full(ids.shape, sigma_ref[0], F32)
    for g in range(1, sigma_ref.shape[0]):
        sigma = jnp.where(ids == g, sigma_ref[g], sigma)
    weights = 1.0 / (sigma * sigma)
    weights_out[...] = jnp.broadcast_to(weights, weights_out.shape)
    weighted = (weights * obs_ref[...]).astype(BF16)
    obs_out[...] = jnp.broadcast_to(weighted, obs_out.shape)


def weigh(observations, group_ids, group_sigma):
    points = observations.shape[0]
    flat = pl.BlockSpec((1, points), lambda i: (0, 0))
    return pl.pallas_call(
        weigh_kernel,
        grid=(1,),
        out_shape=(
            jax.ShapeDtypeStruct((8, points), F32),
            jax.ShapeDtypeStruct((TAIL, points), BF16),
        ),
        in_specs=[IN_SMEM, flat, flat],
        out_specs=[IN_VMEM, IN_VMEM],
        compiler_params=pltpu.CompilerParams(vmem_limit_bytes=2 * 2**20),
    )(group_sigma, observations.reshape(1, -1), group_ids.reshape(1, -1))


def pair_kernel(first_ref, second_ref, out_ref):
    e = pl.program_id(0)
    for half in range(2):
        lanes = slice(half * ROWS, (half + 1) * ROWS)
        out_ref[2 * e + half] = jnp.concatenate(
            [first_ref[:, lanes], second_ref[:, lanes]], axis=1
        )


def pair_up(design_rows):
    points = design_rows.shape[0]
    return pl.pallas_call(
        pair_kernel,
        grid=(NZ // 2,),
        out_shape=jax.ShapeDtypeStruct((NZ, points, PAIR), BF16),
        in_specs=[
            pl.BlockSpec((points, PAIR), lambda e: (0, e)),
            pl.BlockSpec((points, PAIR), lambda e: (0, e + NZ // 2)),
        ],
        out_specs=IN_VMEM,
        compiler_params=pltpu.CompilerParams(vmem_limit_bytes=12 * 2**20),
        cost_estimate=pl.CostEstimate(
            flops=0, bytes_accessed=4 * design_rows.size, transcendentals=0
        ),
    )(design_rows, design_rows)


def collect_kernel(weights_ref, obs_ref, *refs):
    weights = weights_ref[:1, :]
    out, at = refs[-1], 0
    for ref in refs[:-1]:
        value = weights * ref[...].astype(F32)
        out[at : at + ref.shape[0], :] = value.astype(BF16)
        at += ref.shape[0]
    out[at:, :] = obs_ref[...]


def collect(weights, weighted_obs, blocks, after):
    rows = sum(b.shape[0] for b in blocks) + weighted_obs.shape[0]
    return call(
        collect_kernel,
        [jax.ShapeDtypeStruct((rows, weights.shape[1]), BF16)],
        (weights, weighted_obs, *blocks),
        after,
        cost=1e9,
    )[0]


def product(left, right):
    return jnp.dot(left, right, preferred_element_type=F32)


def plus(total, received):
    return total + received[...].astype(F32)


def plus_tailed(total, received):
    main = total[:-TAIL] + received[:-TAIL, :].astype(F32)
    tail = received[-TAIL:, :].astype(F32)
    more = tail[: TAIL // 2] + tail[TAIL // 2 :]
    return jnp.concatenate([main, total[-TAIL:] + jnp.concatenate([more, more], axis=0)], axis=0)


def split(value):
    high = value.astype(BF16).astype(F32)
    return high, value - high


def packed(total):
    high, low = split(total[-TAIL // 2 :])
    return jnp.concatenate([total[:-TAIL], high, low], axis=0).astype(BF16)


def place(dz):
    return (lax.axis_index("rep") + dz) & (NZ - 1)


def x_place():
    return lax.axis_index("rep") >> 3


def x_rows(panel_ref, which):
    at = pl.multiple_of(which * PART, PART)
    return jnp.concatenate([panel_ref[pl.ds(at, PART), :], panel_ref[HALF:, :]], axis=0)


def z_first_kernel(rows_ref, panel_ref, down, up):
    total = product(panel_ref[:HALF, :], rows_ref[place(NZ // 2)]).astype(BF16)
    down[...] = total[: HALF // 2]
    up[...] = total[HALF // 2 :]


def z_first(rows, panel, after):
    return call(
        z_first_kernel,
        [jax.ShapeDtypeStruct((HALF // 2, PAIR), BF16)] * 2,
        (rows, panel),
        after,
        cost=3000000000.0,
    )


def z_product_kernel(steps, rows_ref, panel_ref, *outs):
    left = panel_ref[:HALF, :]
    for out, dz in zip(outs, steps):
        out[...] = product(left, rows_ref[place(dz)])


def z_product(rows, panel, steps, after):
    return call(
        functools.partial(z_product_kernel, steps),
        [jax.ShapeDtypeStruct((HALF, PAIR), F32)] * len(steps),
        (rows, panel),
        after,
        cost=1000000000.0,
    )


def z_add_kernel(*refs):
    n = len(refs) // 3
    for i, (ready, received, out) in enumerate(zip(refs[:n], refs[n : 2 * n], refs[2 * n :])):
        count = received.shape[0]
        if count == HALF:
            out[...] = plus(ready[...], received).astype(BF16)
            continue
        low = slice(0, count) if i == 0 else slice(HALF - count, HALF)
        rest = slice(count, HALF) if i == 0 else slice(0, HALF - count)
        out[low, :] = plus(ready[low, :], received).astype(BF16)
        out[rest, :] = ready[rest, :].astype(BF16)


def z_step(ready, received, after):
    return call(
        z_add_kernel,
        [jax.ShapeDtypeStruct((HALF, PAIR), BF16)] * 2,
        (*ready, *received),
        after,
        cost=2500000000.0,
    )


def over_kernel(steps, rows_ref, panel_ref, out_ref):
    left = x_rows(panel_ref, 1 - x_place())
    for i, dz in enumerate(steps):
        out_ref[i] = packed(product(left, rows_ref[place(dz)]))


def over_x(rows, panel, steps, after):
    return call(
        functools.partial(over_kernel, steps),
        [jax.ShapeDtypeStruct((len(steps), PART + TAIL, PAIR), BF16)],
        (rows, panel),
        after,
        cost=1500000000.0,
    )


def x_kernel(steps, picks, n_over, rows_ref, panel_ref, *refs):
    over, refs = refs[:n_over], refs[n_over:]
    received, outs = refs[: -len(steps)], refs[-len(steps) :]
    left = x_rows(panel_ref, x_place())
    for i, dz in enumerate(steps):
        total = product(left, rows_ref[place(dz)])
        which, at = picks[i]
        total = plus_tailed(total, over[which].at[at])
        if i < len(received):
            total = plus_tailed(total, received[i])
        outs[i][...] = packed(total)


def x_step(rows, panel, steps, over, received, after):
    arrays, picks = [], []
    for dz in steps:
        array, at = over[dz]
        known = [a is array for a in arrays]
        if not any(known):
            known.append(True)
            arrays.append(array)
        picks.append((known.index(True), at))
    return call(
        functools.partial(x_kernel, steps, tuple(picks), len(arrays)),
        [jax.ShapeDtypeStruct((PART + TAIL, PAIR), BF16)] * len(steps),
        (rows, panel, *arrays, *received),
        after,
        cost=3000000000.0,
    )


def halves(total):
    cols = total.shape[0]
    return [
        jnp.concatenate([total[c : c + 64] for c in range(first, cols, 128)], axis=0).T
        for first in (0, 64)
    ]


def own_and_theirs():
    side = x_place()
    return (
        pl.ds(pl.multiple_of(side * ROWS, ROWS), ROWS),
        pl.ds(pl.multiple_of((1 - side) * ROWS, ROWS), ROWS),
    )


def ahead_kernel(at, rows_ref, near_ref, other_ref, over, ready_x, ready_z):
    right = rows_ref[place(0)]
    ready_x[...] = plus_tailed(product(x_rows(near_ref, x_place()), right), over.at[at])
    ready_z[...] = product(other_ref[:HALF, :], right)


def last_ahead(rows, near, other, over, after):
    array, at = over
    return call(
        functools.partial(ahead_kernel, at),
        [
            jax.ShapeDtypeStruct((PART + TAIL, PAIR), F32),
            jax.ShapeDtypeStruct((HALF, PAIR), F32),
        ],
        (rows, near, other, array),
        after,
        cost=1e9,
    )


def z_last_kernel(ready, z_down, z_up, own, beside, cross, across, this, that):
    this[...], that[...] = halves(plus(plus(ready[...], z_down), z_up))
    mine, theirs = own_and_theirs()
    own[...] = this[mine, :]
    beside[...] = this[theirs, :].astype(BF16)
    cross[...] = that[theirs, :].astype(BF16)
    across[...] = that[mine, :].astype(BF16)


def z_last(ready, z_got):
    message = jax.ShapeDtypeStruct((ROWS, PART), BF16)
    return call(
        z_last_kernel,
        [jax.ShapeDtypeStruct((ROWS, PART), F32), message, message, message],
        (ready, *z_got),
        scratch=[pltpu.VMEM((PAIR, PART), F32)] * 2,
        cost=3e9,
    )


def x_last_kernel(ready, z_beside, up, down, own, rhs, beside, cross, across, this, that):
    side = x_place()
    total = plus_tailed(plus_tailed(ready[...], up), down)
    this[...], that[...] = halves(total[:PART])
    mine, theirs = own_and_theirs()
    own[...] = this[mine, :]
    for out, value in (
        (beside, this[theirs, :]),
        (cross, that[theirs, :]),
        (across, that[mine, :]),
    ):
        out[:ROWS, :PART] = jnp.concatenate(split(value), axis=1).astype(BF16)
    beside[:, PART:] = z_beside[...]
    tail = total[PART:]
    lower, upper = tail[: TAIL // 2, :ROWS], tail[: TAIL // 2, ROWS:]
    rhs[...] = jnp.where(side == 0, lower, upper)
    sent = jnp.concatenate(split(jnp.where(side == 0, upper, lower)), axis=0)
    zeros = jnp.zeros((TAIL, PART - ROWS), F32)
    cross[ROWS:, :] = jnp.concatenate([sent, zeros], axis=1).astype(BF16)


def x_last(ready, z_beside, x_got, after):
    return call(
        x_last_kernel,
        [
            jax.ShapeDtypeStruct((ROWS, PART // 2), F32),
            jax.ShapeDtypeStruct((TAIL // 2, ROWS), F32),
            jax.ShapeDtypeStruct((ROWS, HALF), BF16),
            jax.ShapeDtypeStruct((ROWS + TAIL, PART), BF16),
            jax.ShapeDtypeStruct((ROWS, PART), BF16),
        ],
        (ready, z_beside, *x_got),
        after,
        cost=8e9,
        scratch=[pltpu.VMEM((PAIR, PART // 2), F32)] * 2,
    )


def foreign_kernel(first, second, out):
    out[...] = plus(first[...].astype(F32), second)


def foreign_z(first, second, after):
    return call(
        foreign_kernel,
        [jax.ShapeDtypeStruct(first.shape, F32)],
        (first, second),
        after,
        cost=3e9,
    )[0]


def whole(message_ref):
    value = message_ref[:ROWS, :PART].astype(F32)
    return value[:, : PART // 2] + value[:, PART // 2 :]


def finish_kernel(
    own_x, own_z, rhs_ref, there_z, beside, cross, across, out_ref, rhs_out
):
    side, row, half = x_place(), lax.axis_index("row"), lax.axis_index("col")
    y, core = row >> 1, row & 1
    beside_z = beside[:, PART:].astype(F32)
    for where_to, here, there, other in (
        (half, own_x[...], whole(beside), own_z[...] + beside_z),
        (1 - half, whole(across), whole(cross), there_z[...]),
    ):
        near = jnp.concatenate(
            [jnp.where(side == 0, here, there), jnp.where(side == 0, there, here)], axis=1
        )
        first = jnp.where(core == 0, near, other)
        second = jnp.where(core == 0, other, near)
        for dy in range(4):
            lanes = slice(dy * 64, dy * 64 + 64)
            at = pl.multiple_of(((y + dy) & 3) * 128, 128)
            out_ref[0, where_to, :, pl.ds(at, 128)] = jnp.concatenate(
                [first[:, lanes], second[:, lanes]], axis=1
            )
    tail = cross[ROWS:, :].astype(F32)[:, :ROWS]
    mine = rhs_ref[...][:1]
    other = (tail[: TAIL // 2] + tail[TAIL // 2 :])[:1]
    rhs_out[0] = jnp.concatenate(
        [jnp.where(half == 0, mine, other), jnp.where(half == 0, other, mine)], axis=0
    )


def finish(*args):
    return call(
        finish_kernel,
        [
            jax.ShapeDtypeStruct((1, 2, ROWS, HALF), F32),
            jax.ShapeDtypeStruct((1, 2, ROWS), F32),
        ],
        args,
    )


def z_shift(x, d):
    return lax.ppermute(
        x, "rep", [(a * NZ + z, a * NZ + (z + d) % NZ) for a in range(2) for z in range(NZ)]
    )


def x_swap(x):
    return lax.ppermute(
        x, "rep", [(a * NZ + z, (1 - a) * NZ + z) for a in range(2) for z in range(NZ)]
    )


def y_shift(x, d):
    return lax.ppermute(
        x, "row", [(y * 2 + c, (y + d) % 4 * 2 + c) for y in range(4) for c in range(2)]
    )


def core_swap(x):
    return lax.ppermute(x, "row", [(i, i ^ 1) for i in range(8)])


def half_swap(x):
    return lax.ppermute(x, "col", [(0, 1), (1, 0)])


def cross_swap(x):
    pairs = []
    for a in range(2):
        for z in range(NZ):
            for h in range(2):
                pairs.append(((a * NZ + z) * 2 + h, ((1 - a) * NZ + z) * 2 + 1 - h))
    return lax.ppermute(x, ("rep", "col"), pairs)


def per_device(design_rows, design_panel, observations, group_ids, group_sigma):
    points = design_rows.shape[0]
    mine = jnp.transpose(design_panel.reshape(points, -1))
    weights, weighted_obs = weigh(observations, group_ids, group_sigma)
    rows = pair_up(design_rows)

    foreign = half_swap(mine)
    blocks = [mine, foreign]
    for d in (1, 2, 3):
        blocks.append(y_shift(mine, -d))
    for d in (1, 2, 3):
        blocks.append(y_shift(foreign, -d))
    blocks = [blocks[i] for i in (0, 1, 2, 5, 3, 6, 4, 7)]
    near = collect(weights, weighted_obs, blocks, (rows,))
    other = core_swap(near)

    over, z_got, x_got, ready, after = {}, (), (), (), ()

    def piece(*steps):
        nonlocal after
        (sent,) = over_x(rows, near, steps, after)
        after = (sent,)
        got = x_swap(sent)
        for i, dz in enumerate(steps):
            over[dz] = (got, i)

    def z_ahead(s):
        nonlocal after, ready
        ready = z_product(rows, other, (-s, s), after)
        after = (ready[0],)

    def z_next(s):
        nonlocal after, z_got
        if s == NZ // 2:
            sent = z_first(rows, other, after)
        else:
            sent = z_step(ready, z_got, after)
        after = (sent[0],)
        z_got = (z_shift(sent[0], -1), z_shift(sent[1], 1))

    def x_next(s):
        nonlocal after, x_got
        steps = (s,) if s == 4 else (s, -s)
        sent = x_step(rows, near, steps, over, x_got, after)
        after = (sent[0],)
        x_got = (z_shift(sent[0], 1),) + tuple(z_shift(v, -1) for v in sent[1:])

    piece(4)
    z_next(4)
    piece(3, -3)
    x_next(4)
    z_ahead(3)
    z_next(3)
    x_next(3)
    piece(2, -2)
    z_ahead(2)
    z_next(2)
    piece(1, -1, 0)
    x_next(2)
    z_ahead(1)
    z_next(1)
    x_next(1)
    ready_x, ready_z = last_ahead(rows, near, other, over[0], after)
    own_z, beside_z, cross_z, across_z = z_last(ready_z, z_got)
    across_z, cross_z = half_swap(across_z), cross_swap(cross_z)
    own_x, rhs_own, beside, cross, across = x_last(ready_x, beside_z, x_got, (own_z,))
    there_z = foreign_z(cross_z, across_z, (own_x,))
    return finish(
        own_x, own_z, rhs_own, there_z, x_swap(beside), cross_swap(cross), half_swap(across)
    )


def solution(mesh):
    in_specs = (P("rep", ("row", "col")), P("rep", "col", "row"), P("rep"), P("rep"), P())
    out_specs = (P("row", None, "rep", "col"), P("row", None, "rep"))
    return jax.shard_map(
        per_device, mesh=mesh, in_specs=in_specs, out_specs=out_specs, check_vma=False
    )
```
